256 devices in a mesh: dp: 8 (over x, z_hi), seq: 32 (over y, z_lo, core).
Axes of the slice: x: 4, y: 4, z: 8 (z_hi: 2, z_lo: 4; z = z_hi * 4 + z_lo), core: 2. Of those that a mesh axis runs over, the one named last changes fastest.
Arguments:
- tokens: bfloat16 [8, 8192, 1536], P('dp', 'seq'), may hold values from -6 to 6
- pair_in: bfloat16 [8, 512, 512, 128], P('dp', 'seq'), may hold values from -6 to 6
- cotangent: bfloat16 [8, 512, 512, 128], P('dp', 'seq'), may hold values from -6 to 6
- kernel: bfloat16 [32, 1536], replicated, may hold values from -1 to 1
- norm_gain: float32 [1536], replicated, may hold values from 0.1 to 1.9
- left_weight: bfloat16 [1536, 128], replicated, may hold values from -0.15625 to 0.15625
- right_weight: bfloat16 [1536, 128], replicated, may hold values from -0.15625 to 0.15625
- transition_a: bfloat16 [128, 512], replicated, may hold values from -0.5 to 0.5
- transition_b: bfloat16 [512, 128], replicated, may hold values from -0.25 to 0.25
Outputs:
- grad_tokens: bfloat16 [8, 8192, 1536], P('dp', 'seq')
- grad_pair: bfloat16 [8, 512, 512, 128], P('dp', 'seq')
- grad_left_w: float32 [1536, 128], replicated
- grad_right_w: float32 [1536, 128], replicated
- grad_kernel: float32 [32, 1536], replicated
- grad_gain: float32 [1536], replicated
- grad_wa: float32 [128, 512], replicated
- grad_wb: float32 [512, 128], replicated
The draws below stay inside these ranges and needn't reach their ends.
All inputs are finite; a program needn't handle non-finite values.
Results may differ from the reference program's by a relative error of at most 0.02.
Values may be sent and summed in bfloat16 or wider, within the bound.
A program may use at most 64 MiB of HBM per device.

```python
import math
import jax
import jax.numpy as jnp
from jax import lax

C = 1536
PC = 128
PH = 512
POOL = 16
TAPS = 32
BATCH = 8
SEQLEN = 8192
PLEN = 512


def shard_levels(stream_key, dims, cuts, least, largest):
    loudness = 1.0
    for axis_at, shards_of in cuts:
        draws = jax.random.uniform(jax.random.fold_in(jax.random.fold_in(stream_key, 6), axis_at), (shards_of,), jnp.float32, least / len(cuts), largest / len(cuts))
        loudness = loudness * jnp.repeat(jnp.exp(draws), dims[axis_at] // shards_of).reshape((-1,) + (1,) * (len(dims) - 1 - axis_at))
    return loudness


def noise(own_key, shape, spread, limit, pieces=(), held_as=jnp.bfloat16):
    values = spread * jax.random.normal(own_key, shape, jnp.float32)
    if pieces:
        values = values * shard_levels(own_key, shape, pieces, -0.22, 0.18)
    return jnp.clip(values, -limit, limit).astype(held_as)


def setup_inputs(seed: int = 0) -> dict:
    key_of = jax.random.split(jax.random.key(seed), 10)
    return {
        "tokens": noise(key_of[0], (BATCH, SEQLEN, C), 1.0, 6.0, ((0, 8), (1, 32))),
        "pair_in": noise(key_of[1], (BATCH, PLEN, PLEN, PC), 1.0, 6.0, ((0, 8), (1, 32))),
        "cotangent": noise(key_of[2], (BATCH, PLEN, PLEN, PC), 1.0, 6.0, ((0, 8), (1, 32))),
        "kernel": noise(key_of[3], (TAPS, C), TAPS ** -0.5, 1.0),
        "norm_gain": jnp.clip(1.0 + 0.18 * jax.random.normal(key_of[4], (C,), jnp.float32), 0.1, 1.9),
        "left_weight": noise(key_of[5], (C, PC), C ** -0.5, 0.15625),
        "right_weight": noise(key_of[6], (C, PC), C ** -0.5, 0.15625),
        "transition_a": noise(key_of[7], (PC, PH), PC ** -0.5, 0.5),
        "transition_b": noise(key_of[8], (PH, PC), PH ** -0.5, 0.25),
    }


def rms_scale(pooled, norm_gain):
    inverse = lax.rsqrt(lax.optimization_barrier(jnp.mean(pooled * pooled, axis=-1, keepdims=True)) + 1e-06)
    return pooled * inverse * norm_gain

def contract_rows(first_arr, second_arr):
    return lax.dot_general(first_arr, second_arr, (((0,), (0,)), ((), ())), preferred_element_type=jnp.float32)

def pool_tokens(padded, kernel, seq_tokens):
    channels = padded.shape[-1]
    front_taps = padded[:seq_tokens].astype(jnp.float32).reshape(-1, POOL, channels)
    back_taps = padded[POOL:POOL + seq_tokens].astype(jnp.float32).reshape(-1, POOL, channels)
    kernel_f = kernel.astype(jnp.float32)
    pooled = lax.optimization_barrier(jnp.sum(front_taps * kernel_f[:POOL], axis=1)) + lax.optimization_barrier(jnp.sum(back_taps * kernel_f[POOL:], axis=1))
    return (pooled, front_taps, back_taps)

def make_sym(pair_rows, pair_cols, left_rows, right_rows, left_all, right_all):
    outer = left_rows.astype(jnp.float32)[:, None, :] * right_all.astype(jnp.float32)[None]
    outer = outer + right_rows.astype(jnp.float32)[:, None, :] * left_all.astype(jnp.float32)[None]
    return (pair_rows.astype(jnp.float32) + pair_cols.astype(jnp.float32) + outer).astype(jnp.bfloat16)

def transition_back(sym_rows, cot_rows, transition_a, transition_b, weights_too):
    preact = jnp.dot(sym_rows, transition_a, preferred_element_type=jnp.float32)
    sigmoid_pre = jax.nn.sigmoid(preact)
    grad_act = jnp.dot(cot_rows, transition_b.T, preferred_element_type=jnp.float32)
    grad_pre = (grad_act * sigmoid_pre * (1.0 + preact * (1.0 - sigmoid_pre))).astype(jnp.bfloat16)
    grad_sym = cot_rows.astype(jnp.float32) + jnp.dot(grad_pre, transition_a.T, preferred_element_type=jnp.float32)
    if weights_too:
        activation = (preact * sigmoid_pre).astype(jnp.bfloat16)
        return (grad_sym, contract_rows(sym_rows, grad_pre), contract_rows(activation, cot_rows))
    return grad_sym

def spread_back(extended, kernel, pair_count):
    kernel_f = kernel.astype(jnp.float32)
    grad_f = extended.astype(jnp.float32)
    half_pool = POOL // 2
    lower_half = grad_f[1:pair_count + 1, None] * kernel_f[half_pool:POOL] + grad_f[0:pair_count, None] * kernel_f[POOL + half_pool:]
    upper_half = grad_f[2:pair_count + 2, None] * kernel_f[:half_pool] + grad_f[1:pair_count + 1, None] * kernel_f[POOL:POOL + half_pool]
    joined = jnp.concatenate([lower_half, upper_half], axis=1)
    return joined.reshape(pair_count * POOL, -1).astype(jnp.bfloat16)

def kernel_grad(grad_pooled, front_taps, back_taps):
    grad_f = grad_pooled.astype(jnp.float32)[:, None]
    return jnp.concatenate([lax.optimization_barrier(jnp.sum(grad_f * front_taps, axis=0)), lax.optimization_barrier(jnp.sum(grad_f * back_taps, axis=0))], axis=0)

def one_sequence(tokens_seq, pair_seq, cot_seq, kernel, norm_gain, left_weight, right_weight, transition_a, transition_b):
    seq_tokens = tokens_seq.shape[0]
    half_pool = POOL // 2
    padded = jnp.pad(tokens_seq, ((half_pool, half_pool), (0, 0)))
    pooled, front_taps, back_taps = pool_tokens(padded, kernel, seq_tokens)
    normed_f, norm_back = jax.vjp(rms_scale, pooled, norm_gain)
    normed = normed_f.astype(jnp.bfloat16)
    left_proj = jnp.dot(normed, left_weight, preferred_element_type=jnp.float32).astype(jnp.bfloat16)
    right_proj = jnp.dot(normed, right_weight, preferred_element_type=jnp.float32).astype(jnp.bfloat16)
    plen = pooled.shape[0]
    pair_channels = pair_seq.shape[-1]
    block_rows = math.gcd(plen, 16)
    count = plen // block_rows

    def row_block(block_index):
        first_row = block_index * block_rows
        pair_rows = lax.dynamic_slice_in_dim(pair_seq, first_row, block_rows, 0)
        pair_cols = jnp.swapaxes(lax.dynamic_slice_in_dim(pair_seq, first_row, block_rows, 1), 0, 1)
        cot_rows = lax.dynamic_slice_in_dim(cot_seq, first_row, block_rows, 0)
        left_rows = lax.dynamic_slice_in_dim(left_proj, first_row, block_rows, 0)
        right_rows = lax.dynamic_slice_in_dim(right_proj, first_row, block_rows, 0)
        sym = make_sym(pair_rows, pair_cols, left_rows, right_rows, left_proj, right_proj)
        grad_sym, grad_wa, grad_wb = transition_back(sym.reshape(-1, pair_channels), cot_rows.reshape(-1, pair_channels), transition_a, transition_b, True)
        return (grad_sym.astype(jnp.bfloat16).reshape(block_rows, plen, pair_channels), grad_wa, grad_wb)
    grad_sym_all, wa_parts, wb_parts = lax.map(row_block, jnp.arange(count, dtype=jnp.int32))
    grad_sym_all = grad_sym_all.reshape(plen, plen, pair_channels)
    grad_full = grad_sym_all.astype(jnp.float32) + jnp.swapaxes(grad_sym_all, 0, 1).astype(jnp.float32)
    grad_left = lax.optimization_barrier(jnp.sum(grad_full * right_proj.astype(jnp.float32)[None], axis=1)).astype(jnp.bfloat16)
    grad_right = lax.optimization_barrier(jnp.sum(grad_full * left_proj.astype(jnp.float32)[:, None], axis=0)).astype(jnp.bfloat16)
    grad_normed = jnp.dot(grad_left, left_weight.T, preferred_element_type=jnp.float32) + jnp.dot(grad_right, right_weight.T, preferred_element_type=jnp.float32)
    grad_pooled_f, grad_gain = norm_back(grad_normed)
    grad_pooled = grad_pooled_f.astype(jnp.bfloat16)
    extended = jnp.pad(grad_pooled, ((1, 1), (0, 0)))
    grad_tokens = spread_back(extended, kernel, plen)
    grad_kern = kernel_grad(grad_pooled, front_taps, back_taps)
    return (grad_tokens, grad_full.astype(jnp.bfloat16), contract_rows(normed, grad_left), contract_rows(normed, grad_right), grad_kern, grad_gain, lax.optimization_barrier(jnp.sum(wa_parts, axis=0)), lax.optimization_barrier(jnp.sum(wb_parts, axis=0)))

def reference(tokens, pair_in, cotangent, kernel, norm_gain, left_weight, right_weight, transition_a, transition_b):

    def per_sequence(batch_items):
        return one_sequence(batch_items[0], batch_items[1], batch_items[2], kernel, norm_gain, left_weight, right_weight, transition_a, transition_b)
    results = lax.map(per_sequence, (tokens, pair_in, cotangent))
    grad_scale = 1.0 / math.sqrt(BATCH * PLEN * PLEN)
    return (results[0], results[1], lax.optimization_barrier(jnp.sum(results[2], axis=0)) * grad_scale, lax.optimization_barrier(jnp.sum(results[3], axis=0)) * grad_scale, lax.optimization_barrier(jnp.sum(results[4], axis=0)) * grad_scale, lax.optimization_barrier(jnp.sum(results[5], axis=0)) * grad_scale, lax.optimization_barrier(jnp.sum(results[6], axis=0)) * grad_scale, lax.optimization_barrier(jnp.sum(results[7], axis=0)) * grad_scale)
```

```python
import functools
import math

import jax
import jax.numpy as jnp
from jax import lax
from jax.experimental import pallas as pl
from jax.experimental.pallas import tpu as pltpu
from jax.sharding import PartitionSpec as P

POOL = 16
NB = 12
F32 = jnp.float32
BF16 = jnp.bfloat16
MESH = pl.DeviceIdType.MESH


def dot(a, b, ca, cb):
    return lax.dot_general(a, b, (((ca,), (cb,)), ((), ())), preferred_element_type=F32)


def body(
    scale,
    tokens,
    pair,
    cot,
    taps,
    gain,
    lw,
    rw,
    wa,
    wb,
    g_tokens,
    g_pair,
    g_lw,
    g_rw,
    g_taps,
    g_gain,
    g_wa,
    g_wb,
    tokv,
    gtokv,
    pairv,
    cotv,
    recv,
    obuf,
    rbuf,
    feats,
    perm,
    wcat,
    cen,
    up,
    dn,
    normed,
    gpx,
    halo_out,
    halo_in,
    accl,
    accr,
    wacc,
    acc,
    send_a,
    recv_a,
    send_b,
    recv_b,
    mid,
    recv_c,
    fin,
    gat,
    loc,
    osem,
    tile_s,
    tile_r,
    feat_s,
    feat_r,
    ret_s,
    ret_r,
    halo_s,
    halo_r,
    a_s,
    a_r,
    b_s,
    b_r,
    c_s,
    c_r,
    f_s,
    f_r,
    d_s,
    d_r,
    e_s,
    e_r,
):
    dpi = lax.axis_index("dp")
    me = lax.axis_index("seq")
    x, zh = lax.div(dpi, 2), lax.rem(dpi, 2)
    chip, core = lax.div(me, 2), lax.rem(me, 2)
    y, zl = lax.div(chip, 4), lax.rem(chip, 4)
    zz = zh * 4 + zl
    partner = chip * 2 + 1 - core

    def step(s):
        late = s >= 12
        dy = jnp.where(late, s - 11, lax.div(s, 3))
        dz = jnp.where(late, 0, 1 + lax.rem(s + 1, 3))
        return dy, dz

    def target(s):
        dy, dz = step(s)
        q = lax.rem(y + dy, 4) * 4 + lax.rem(zl + dz, 4)
        return q * 2 + jnp.where(q > chip, core, 1 - core)

    def source(s):
        dy, dz = step(s)
        r = lax.rem(y + 4 - dy, 4) * 4 + lax.rem(zl + 4 - dz, 4)
        return r * 2 + jnp.where(r < chip, core, 1 - core)

    def in_seq(k):
        return (dpi, k)

    def plane(u):
        px, py = lax.rem(x + lax.div(u, 4), 4), lax.rem(y + lax.rem(u, 4), 4)
        return px * 4 + py, (px * 2 + zh, py * 8 + zl * 2 + core)

    def ring(v):
        t = lax.rem(zz + v, 8)
        return t, (x * 2 + lax.div(t, 4), y * 8 + lax.rem(t, 4) * 2 + core)

    def remote(src, dst, ssem, rsem, dev):
        return pltpu.make_async_remote_copy(
            src_ref=src, dst_ref=dst, send_sem=ssem, recv_sem=rsem, device_id=dev, device_id_type=MESH
        )

    def cols(k):
        return pl.ds(pl.multiple_of(k * 16, 16), 16)

    def loop(lo, hi, f):
        def g(i, carry):
            f(i)
            return carry

        lax.fori_loop(lo, hi, g, 0)

    local = [
        pltpu.make_async_copy(tokens, tokv, loc.at[0]),
        pltpu.make_async_copy(lw, wcat.at[:, pl.ds(0, 128)], loc.at[1]),
        pltpu.make_async_copy(rw, wcat.at[:, pl.ds(128, 128)], loc.at[2]),
        pltpu.make_async_copy(pair, pairv, loc.at[3]),
        pltpu.make_async_copy(cot, cotv, loc.at[4]),
        pltpu.make_async_copy(pair.at[:, cols(me), :], recv.at[16, 0], loc.at[5]),
        pltpu.make_async_copy(cot.at[:, cols(me), :], recv.at[16, 1], loc.at[6]),
    ]
    for c in local:
        c.start()

    barrier = pltpu.get_barrier_semaphore()

    def greet(dev):
        pl.semaphore_signal(barrier, inc=1, device_id=dev, device_id_type=MESH)

    def greet_seq(s):
        greet(in_seq(target(s)))
        greet(in_seq(source(s)))

    loop(0, 15, greet_seq)
    greet(in_seq(partner))
    loop(4, 16, lambda u: greet(plane(u)[1]))
    loop(0, 4, lambda v: greet((x * 2 + 1 - zh, y * 8 + v * 2 + core)))
    pl.semaphore_wait(barrier, 47)

    def tile_copy(s, k, dev):
        return remote(
            (pair, cot)[k].at[:, cols(dev), :], recv.at[s, k], tile_s.at[s, k], tile_r.at[s, k], in_seq(dev)
        )

    def send_tile(s):
        dev = target(s)
        tile_copy(s, 0, dev).start()
        tile_copy(s, 1, dev).start()

    loop(0, 15, send_tile)
    tile_copy(15, 0, partner).start()
    tile_copy(15, 1, partner).start()

    row = lax.broadcasted_iota(jnp.int32, (256, 256), 0)
    col = lax.broadcasted_iota(jnp.int32, (256, 256), 1)
    perm[...] = jnp.where(col == (row & 15) * 16 + (row >> 4), 1.0, 0.0).astype(BF16)
    wacc[...] = jnp.zeros_like(wacc)
    accl[...] = jnp.zeros_like(accl)
    accr[...] = jnp.zeros_like(accr)

    def lanes(b):
        return pl.ds(pl.multiple_of(b * 128, 128), 128)

    local[0].wait()

    def tap_parts(b):
        k = taps[:, lanes(b)].astype(F32)
        return k[0:8], k[8:16], k[16:24], k[24:32]

    def pool(b):
        k0, k1, k2, k3 = tap_parts(b)
        for p in range(16):
            t = tokv[p * 16 : p * 16 + 16, lanes(b)].astype(F32)
            lo, hi = t[0:8], t[8:16]
            cen[b, p : p + 1] = jnp.sum(lo * k1 + hi * k2, axis=0, keepdims=True)
            up[b, p + 1 : p + 2] = jnp.sum(hi * k0, axis=0, keepdims=True)
            dn[b, p : p + 1] = jnp.sum(lo * k3, axis=0, keepdims=True)
        halo_out[0, b] = dn[b, 0:1]
        halo_out[1, b] = up[b, 16:17]

    loop(0, NB, pool)
    left, right = lax.rem(me + 31, 32), lax.rem(me + 1, 32)

    def halo(k, j, dev):
        return remote(halo_out.at[k], halo_in.at[k], halo_s.at[k], halo_r.at[k], in_seq(dev))

    def halo_pair(k):
        return halo(k, 0, left), halo(k + 1, 1, right)

    to_left, to_right = halo_pair(0)
    to_left.start()
    to_right.start()
    to_left.wait()
    to_right.wait()
    first = jnp.where(me == 0, 0.0, 1.0)
    last = jnp.where(me == 31, 0.0, 1.0)

    def finish_pool(b, total):
        up[b, 0:1] = halo_in[1, b] * first
        dn[b, 16:17] = halo_in[0, b] * last
        v = cen[b] + up[b, 0:16] + dn[b, 1:17]
        cen[b] = v
        return total + v * v

    squares = lax.fori_loop(0, NB, finish_pool, jnp.zeros((16, 128), F32))
    inv = lax.rsqrt(jnp.sum(squares, axis=1, keepdims=True) / (NB * 128.0) + 1e-6)
    local[1].wait()
    local[2].wait()

    def project(b, total):
        n = (cen[b] * inv * gain[b]).astype(BF16)
        normed[b] = n
        return total + dot(n, wcat[pl.ds(pl.multiple_of(b * 128, 128), 128), :], 1, 0)

    feats[me] = lax.fori_loop(0, NB, project, jnp.zeros((16, 256), F32)).astype(BF16)

    def feat_copy(slot, dev):
        return remote(feats.at[me], feats.at[me], feat_s.at[slot], feat_r.at[me], in_seq(dev))

    def feat_arrived(k):
        remote(feats.at[k], feats.at[k], feat_s.at[31], feat_r.at[k], in_seq(k)).wait_recv()

    def send_feat(s):
        feat_copy(s, source(s)).start()
        feat_copy(15 + s, target(s)).start()

    feat_copy(30, partner).start()
    loop(0, 15, send_feat)

    for c in local[3:]:
        c.wait()

    def out_copy(slot, k):
        return pltpu.make_async_copy(obuf.at[slot], g_pair.at[:, cols(k), :], osem.at[slot])

    def add_left_right(grad, f):
        accl[...] += grad * f[:, 128:][None]
        accr[...] += grad * f[:, :128][None]

    def tile(s, k, weight):
        own = jnp.concatenate(
            [pairv[:, cols(k), :].reshape(256, 128), cotv[:, cols(k), :].reshape(256, 128)], axis=1
        )
        other = jnp.concatenate([recv[s, 0].reshape(256, 128), recv[s, 1].reshape(256, 128)], axis=1)
        both = own.astype(F32) + dot(perm[...], other, 1, 0)
        mine, theirs = feats[me].astype(F32), feats[k].astype(F32)
        outer = mine[:, None, :128] * theirs[None, :, 128:] + mine[:, None, 128:] * theirs[None, :, :128]
        sym = (both[:, :128] + outer.reshape(256, 128)).astype(BF16)
        cs = both[:, 128:]
        csb = cs.astype(BF16)
        pre = dot(sym, wa[...], 1, 0)
        sig = 0.5 * jnp.tanh(0.5 * pre) + 0.5
        act = pre * sig
        gpre = (dot(csb, wb[...], 1, 1) * (sig + act * (1.0 - sig))).astype(BF16)
        grad = cs + dot(gpre, wa[...], 1, 1)
        wacc[0] += dot(sym, gpre, 0, 0) * weight
        wacc[1] += dot(csb, act.astype(BF16), 0, 0) * weight
        add_left_right(grad.reshape(16, 16, 128), theirs)
        gradb = grad.astype(BF16)
        obuf[s] = gradb.reshape(16, 16, 128)
        out_copy(s, k).start()
        return gradb

    tile(16, me, 0.5)
    tile_copy(15, 0, partner).wait()
    tile_copy(15, 1, partner).wait()
    feat_arrived(partner)
    tile(15, partner, 0.5)

    def ret_copy(s, dev):
        return remote(rbuf.at[s], obuf.at[17 + s], ret_s.at[s], ret_r.at[s], in_seq(dev))

    def owned(s):
        k = source(s)
        dev = target(s)
        feat_arrived(k)
        tile_copy(s, 0, dev).wait_recv()
        tile_copy(s, 1, dev).wait_recv()
        gradb = tile(s, k, 1.0)
        rbuf[s] = dot(perm[...], gradb, 1, 0).astype(BF16).reshape(16, 16, 128)
        ret_copy(s, k).start()

    loop(0, 15, owned)

    def returned(s):
        k = target(s)
        feat_arrived(k)
        ret_copy(s, source(s)).wait_recv()
        out_copy(17 + s, k).start()
        add_left_right(obuf[17 + s].astype(F32), feats[k].astype(F32))

    loop(0, 15, returned)

    glr = jnp.concatenate(
        [jnp.sum(accl[...], axis=1).astype(BF16), jnp.sum(accr[...], axis=1).astype(BF16)], axis=1
    )

    def grad_norm(b, carry):
        total, unused = carry
        gn = dot(glr, wcat[pl.ds(pl.multiple_of(b * 128, 128), 128), :], 1, 1)
        scaled = gn * gain[b]
        gpx[b, 1:17] = scaled
        acc[24, 8, pl.ds(b, 1)] = jnp.sum(gn * cen[b] * inv, axis=0, keepdims=True) * scale
        return total + scaled * cen[b], unused

    for g in range(24, 32):
        acc[g, 8] = jnp.zeros((16, 128), F32)
    total, _ = lax.fori_loop(0, NB, grad_norm, (jnp.zeros((16, 128), F32), 0))
    mean = jnp.sum(total, axis=1, keepdims=True) / (NB * 128.0) * inv * inv * inv

    def grad_pool(b):
        v = (gpx[b, 1:17] * inv - cen[b] * mean).astype(BF16).astype(F32)
        gpx[b, 1:17] = v
        halo_out[2, b] = v[0:1]
        halo_out[3, b] = v[15:16]

    loop(0, NB, grad_pool)
    to_left2, to_right2 = halo_pair(2)
    to_left2.start()
    to_right2.start()

    def features_grad(b):
        prod = dot(normed[b], glr, 0, 0) * scale
        acc[b, 0:8] = prod[:, :128].reshape(8, 16, 128)
        acc[b + 12, 0:8] = prod[:, 128:].reshape(8, 16, 128)

    loop(0, NB, features_grad)
    for q in range(4):
        lane = slice(q * 128, q * 128 + 128)
        acc[24 + q, 0:8] = (wacc[0, :, lane] * scale).reshape(8, 16, 128)
        acc[28 + q, 0:8] = (wacc[1, :, lane].T * scale).reshape(8, 16, 128)

    to_left2.wait()
    to_right2.wait()

    def token_grad(b):
        k0, k1, k2, k3 = tap_parts(b)
        gpx[b, 0:1] = halo_in[3, b] * first
        gpx[b, 17:18] = halo_in[2, b] * last
        s0 = s1 = s2 = s3 = jnp.zeros((8, 128), F32)
        for p in range(16):
            before, here, after = gpx[b, p : p + 1], gpx[b, p + 1 : p + 2], gpx[b, p + 2 : p + 3]
            t = tokv[p * 16 : p * 16 + 16, lanes(b)].astype(F32)
            lo, hi = t[0:8], t[8:16]
            s0 = s0 + after * hi
            s1 = s1 + here * lo
            s2 = s2 + here * hi
            s3 = s3 + before * lo
            g = jnp.concatenate([here * k1 + before * k3, here * k2 + after * k0], axis=0)
            gtokv[p * 16 : p * 16 + 16, lanes(b)] = g.astype(BF16)
        acc[2 * b, 8, 0:8] = s0 * scale
        acc[2 * b, 8, 8:16] = s1 * scale
        acc[2 * b + 1, 8, 0:8] = s2 * scale
        acc[2 * b + 1, 8, 8:16] = s3 * scale

    loop(0, NB, token_grad)
    tok_out = pltpu.make_async_copy(gtokv, g_tokens, loc.at[7])
    tok_out.start()

    def a_copy(j):
        return remote(send_a.at[j], recv_a.at[j], a_s.at[j], a_r.at[j], in_seq(partner))

    def to_partner(u):
        j = plane(u)[0]
        send_a[j] = acc[(1 - core) * 16 + j].astype(BF16)
        a_copy(j).start()

    loop(0, 16, to_partner)

    def b_copy(u, dev):
        return remote(send_b.at[u], recv_b.at[u], b_s.at[u], b_r.at[u], dev)

    jme = x * 4 + y
    a_copy(jme).wait_recv()
    mid[...] = acc[core * 16 + jme] + recv_a[jme].astype(F32)

    def to_plane(u):
        j, dev = plane(u)
        a_copy(j).wait_recv()
        send_b[u] = (acc[core * 16 + j] + recv_a[j].astype(F32)).astype(BF16)
        b_copy(u, dev).start()

    loop(1, 16, to_plane)

    def from_plane(u):
        b_copy(u, plane(u)[1]).wait_recv()
        mid[...] += recv_b[u].astype(F32)

    loop(1, 16, from_plane)

    def c_copy(t, dev, slot):
        return (
            remote(mid.at[t], recv_c.at[slot, 0], c_s.at[t, 0], c_r.at[slot, 0], dev),
            remote(mid.at[8], recv_c.at[slot, 1], c_s.at[t, 1], c_r.at[slot, 1], dev),
        )

    def to_ring(v):
        t, dev = ring(v)
        for c in c_copy(t, dev, zz):
            c.start()

    loop(1, 8, to_ring)
    recv_c[zz, 0] = mid[zz]
    recv_c[zz, 1] = mid[8]

    def from_ring(v):
        t, dev = ring(v)
        for c in c_copy(t, dev, t):
            c.wait_recv()

    loop(1, 8, from_ring)
    summed = recv_c[0]
    for t in range(1, 8):
        summed = summed + recv_c[t]
    fin[zz] = summed[0].astype(BF16)
    fin[8] = summed[1].astype(BF16)

    def f_copy(slot, v, dev):
        return remote(fin.at[slot], fin.at[slot], f_s.at[v], f_r.at[slot], dev)

    loop(1, 8, lambda v: f_copy(zz, v, ring(v)[1]).start())
    loop(1, 8, lambda v: f_copy(ring(v)[0], v, ring(v)[1]).wait_recv())

    def d_copy(u, dev, j):
        return remote(fin, gat.at[core * 16 + j], d_s.at[u], d_r.at[j], dev)

    loop(1, 16, lambda u: d_copy(u, plane(u)[1], jme).start())
    gat[core * 16 + jme] = fin[...]

    def e_copy(j, half):
        slot = gat.at[half * 16 + j]
        return remote(slot, slot, e_s.at[j], e_r.at[j], in_seq(partner))

    e_copy(jme, core).start()

    def forward(u):
        j, dev = plane(u)
        d_copy(u, dev, j).wait_recv()
        e_copy(j, core).start()

    loop(1, 16, forward)
    loop(0, 16, lambda j: e_copy(j, 1 - core).wait_recv())

    for b in range(NB):
        rows = slice(b * 128, b * 128 + 128)
        g_lw[rows, :] = gat[b, 0:8].reshape(128, 128).astype(F32)
        g_rw[rows, :] = gat[b + 12, 0:8].reshape(128, 128).astype(F32)
        g_taps[0:16, rows] = gat[2 * b, 8].astype(F32)
        g_taps[16:32, rows] = gat[2 * b + 1, 8].astype(F32)
    gains = gat[24, 8].astype(F32)
    for b in range(NB):
        g_gain[:, b * 128 : b * 128 + 128] = gains[b : b + 1]
    for q in range(4):
        lane = slice(q * 128, q * 128 + 128)
        g_wa[:, lane] = gat[24 + q, 0:8].reshape(128, 128).astype(F32)
        g_wb[lane, :] = gat[28 + q, 0:8].reshape(128, 128).astype(F32)

    def drain_tile(s):
        dev = target(s)
        tile_copy(s, 0, dev).wait_send()
        tile_copy(s, 1, dev).wait_send()
        feat_copy(s, source(s)).wait_send()
        feat_copy(15 + s, dev).wait_send()
        ret_copy(s, source(s)).wait_send()
        out_copy(17 + s, dev).wait()

    loop(0, 15, drain_tile)
    feat_copy(30, partner).wait_send()
    loop(0, 17, lambda s: out_copy(s, me).wait())
    tok_out.wait()

    def drain_sum(u):
        j, dev = plane(u)
        b_copy(u, dev).wait_send()
        d_copy(u, dev, j).wait_send()

    loop(1, 16, drain_sum)
    loop(0, 16, lambda j: a_copy(j).wait_send())
    loop(0, 16, lambda j: e_copy(j, core).wait_send())

    def drain_ring(v):
        t, dev = ring(v)
        for c in c_copy(t, dev, zz):
            c.wait_send()
        f_copy(zz, v, dev).wait_send()

    loop(1, 8, drain_ring)


def local(tokens, pair_in, cotangent, kernel, norm_gain, left_weight, right_weight, transition_a, transition_b):
    plen = pair_in.shape[2]
    scale = 1.0 / math.sqrt(lax.axis_size("dp") * plen * plen)
    vmem = pl.BlockSpec(memory_space=pltpu.VMEM)
    hbm = pl.BlockSpec(memory_space=pl.ANY)
    dma = pltpu.SemaphoreType.DMA
    tile = (16, 16, 128)
    chunk = (9, 16, 128)
    outs = pl.pallas_call(
        functools.partial(body, scale),
        out_shape=(
            jax.ShapeDtypeStruct((256, 1536), BF16),
            jax.ShapeDtypeStruct((16, 512, 128), BF16),
            jax.ShapeDtypeStruct((1536, 128), F32),
            jax.ShapeDtypeStruct((1536, 128), F32),
            jax.ShapeDtypeStruct((32, 1536), F32),
            jax.ShapeDtypeStruct((1, 1536), F32),
            jax.ShapeDtypeStruct((128, 512), F32),
            jax.ShapeDtypeStruct((512, 128), F32),
        ),
        in_specs=[hbm, hbm, hbm, vmem, vmem, hbm, hbm, vmem, vmem],
        out_specs=(hbm, hbm) + (vmem,) * 6,
        scratch_shapes=[
            pltpu.VMEM((256, 1536), BF16),
            pltpu.VMEM((256, 1536), BF16),
            pltpu.VMEM((16, 512, 128), BF16),
            pltpu.VMEM((16, 512, 128), BF16),
            pltpu.VMEM((17, 2) + tile, BF16),
            pltpu.VMEM((32,) + tile, BF16),
            pltpu.VMEM((15,) + tile, BF16),
            pltpu.VMEM((32, 16, 256), BF16),
            pltpu.VMEM((256, 256), BF16),
            pltpu.VMEM((1536, 256), BF16),
            pltpu.VMEM((NB, 16, 128), F32),
            pltpu.VMEM((NB, 24, 128), F32),
            pltpu.VMEM((NB, 24, 128), F32),
            pltpu.VMEM((NB, 16, 128), BF16),
            pltpu.VMEM((NB, 24, 128), F32),
            pltpu.VMEM((4, NB, 1, 128), F32),
            pltpu.VMEM((4, NB, 1, 128), F32),
            pltpu.VMEM(tile, F32),
            pltpu.VMEM(tile, F32),
            pltpu.VMEM((2, 128, 512), F32),
            pltpu.VMEM((32,) + chunk, F32),
            pltpu.VMEM((16,) + chunk, BF16),
            pltpu.VMEM((16,) + chunk, BF16),
            pltpu.VMEM((16,) + chunk, BF16),
            pltpu.VMEM((16,) + chunk, BF16),
            pltpu.VMEM(chunk, F32),
            pltpu.VMEM((8, 2, 16, 128), F32),
            pltpu.VMEM(chunk, BF16),
            pltpu.VMEM((32,) + chunk, BF16),
            dma((8,)),
            dma((32,)),
            dma((16, 2)),
            dma((16, 2)),
            dma((32,)),
            dma((32,)),
            dma((15,)),
            dma((15,)),
            dma((4,)),
            dma((4,)),
            dma((16,)),
            dma((16,)),
            dma((16,)),
            dma((16,)),
            dma((8, 2)),
            dma((8, 2)),
            dma((8,)),
            dma((8,)),
            dma((16,)),
            dma((16,)),
            dma((16,)),
            dma((16,)),
        ],
        compiler_params=pltpu.CompilerParams(
            collective_id=0, has_side_effects=True, vmem_limit_bytes=48 * 1024 * 1024
        ),
    )(
        tokens[0],
        pair_in[0],
        cotangent[0],
        kernel,
        norm_gain.reshape(NB, 1, 128),
        left_weight,
        right_weight,
        transition_a,
        transition_b,
    )
    return (outs[0][None], outs[1][None], outs[2], outs[3], outs[4], outs[5].reshape(1536), outs[6], outs[7])


def solution(mesh):
    placed = (
        P("dp", "seq", None),
        P("dp", "seq", None, None),
        P("dp", "seq", None, None),
        P(),
        P(),
        P(),
        P(),
        P(),
        P(),
    )
    return jax.shard_map(
        local,
        mesh=mesh,
        in_specs=placed,
        out_specs=(P("dp", "seq", None), P("dp", "seq", None, None), P(), P(), P(), P(), P(), P()),
        check_vma=False,
    )
```

```python
import functools
import math

import jax
import jax.numpy as jnp
from jax import lax
from jax.experimental import pallas as pl
from jax.experimental.pallas import tpu as pltpu
from jax.sharding import PartitionSpec as P

POOL = 16
NB = 12
EARLY = 2
VMEM_LIMIT = 58 * 1024 * 1024
F32 = jnp.float32
BF16 = jnp.bfloat16
MESH = pl.DeviceIdType.MESH


def dot(a, b, ca, cb):
    return lax.dot_general(a, b, (((ca,), (cb,)), ((), ())), preferred_element_type=F32)


def body(
    scale,
    tokens,
    pair,
    cot,
    taps_h,
    gain_h,
    lw,
    rw,
    wa_h,
    wb_h,
    g_tokens,
    g_pair,
    gat,
    gtokv,
    gpair,
    tokv,
    tokh,
    pairv,
    cotv,
    recv,
    rbuf,
    feats,
    perm,
    wcat,
    taps,
    gain,
    wa,
    wb,
    cen,
    up,
    dn,
    normed,
    gpx,
    halo_out,
    halo_in,
    accl,
    accr,
    wacc,
    glr_out,
    nin,
    gin,
    w3_out,
    w3_in,
    w2_out,
    w2_in,
    mid,
    recv_c,
    fin,
    loc,
    tile_s,
    tile_r,
    feat_s,
    feat_r,
    ret_s,
    ret_r,
    halo_s,
    halo_r,
    th_s,
    th_r,
    n_s,
    n_r,
    g_s,
    g_r,
    w3_s,
    w3_r,
    w2_s,
    w2_r,
    c_s,
    c_r,
    f_s,
    f_r,
    d_s,
    d_r,
    e_s,
    e_r,
):
    dpi = lax.axis_index("dp")
    me = lax.axis_index("seq")
    x, zh = lax.div(dpi, 2), lax.rem(dpi, 2)
    chip, core = lax.div(me, 2), lax.rem(me, 2)
    y, zl = lax.div(chip, 4), lax.rem(chip, 4)
    zz = zh * 4 + zl
    partner = chip * 2 + 1 - core

    def step(s):
        late = s >= 12
        dy = jnp.where(late, s - 11, lax.div(s, 3))
        dz = jnp.where(late, 0, 1 + lax.rem(s + 1, 3))
        return dy, dz

    def target(s):
        dy, dz = step(s)
        q = lax.rem(y + dy, 4) * 4 + lax.rem(zl + dz, 4)
        return q * 2 + jnp.where(q > chip, core, 1 - core)

    def source(s):
        dy, dz = step(s)
        r = lax.rem(y + 4 - dy, 4) * 4 + lax.rem(zl + 4 - dz, 4)
        return r * 2 + jnp.where(r < chip, core, 1 - core)

    def in_seq(k):
        return (dpi, k)

    def plane(u):
        px, py = lax.rem(x + lax.div(u, 4), 4), lax.rem(y + lax.rem(u, 4), 4)
        return chunk_of(px, py, core), (px * 2 + zh, py * 8 + zl * 2 + core)

    def chunk_of(px, py, pc):
        odd = lax.rem(px + py, 2)
        return jnp.where(pc == 0, px * 4 + py, 16 + (1 - odd) * 8 + px * 2 + lax.div(py, 2))

    def owner(g):
        t = lax.rem(g, 16)
        e, r = lax.div(t, 8), lax.rem(t, 8)
        rx = lax.div(r, 2)
        ry = lax.rem(r, 2) * 2 + lax.rem(1 - e + rx, 2)
        px = jnp.where(g < 16, lax.div(t, 4), rx)
        py = jnp.where(g < 16, lax.rem(t, 4), ry)
        return (px * 2 + zh, py * 8 + zl * 2 + lax.div(g, 16))

    mine = chunk_of(x, y, core)

    def ring(v):
        t = lax.rem(zz + v, 8)
        return t, (x * 2 + lax.div(t, 4), y * 8 + lax.rem(t, 4) * 2 + core)

    def remote(src, dst, ssem, rsem, dev):
        return pltpu.make_async_remote_copy(
            src_ref=src, dst_ref=dst, send_sem=ssem, recv_sem=rsem, device_id=dev, device_id_type=MESH
        )

    def cols(k):
        return pl.ds(pl.multiple_of(k * 16, 16), 16)

    def loop(lo, hi, f):
        def g(i, carry):
            f(i)
            return carry

        lax.fori_loop(lo, hi, g, 0)

    local = [
        pltpu.make_async_copy(tokens, tokv, loc.at[0]),
        pltpu.make_async_copy(taps_h, taps, loc.at[1]),
        pltpu.make_async_copy(gain_h, gain, loc.at[2]),
        pltpu.make_async_copy(lw, wcat.at[:, pl.ds(0, 128)], loc.at[3]),
        pltpu.make_async_copy(rw, wcat.at[:, pl.ds(128, 128)], loc.at[4]),
        pltpu.make_async_copy(wa_h, wa, loc.at[5]),
        pltpu.make_async_copy(wb_h, wb, loc.at[6]),
        pltpu.make_async_copy(pair, pairv, loc.at[7]),
        pltpu.make_async_copy(cot, cotv, loc.at[8]),
        pltpu.make_async_copy(pair.at[:, cols(me), :], recv.at[16, 0], loc.at[9]),
        pltpu.make_async_copy(cot.at[:, cols(me), :], recv.at[16, 1], loc.at[10]),
    ]
    for c in local:
        c.start()

    barrier = pltpu.get_barrier_semaphore()

    def greet(dev):
        pl.semaphore_signal(barrier, inc=1, device_id=dev, device_id_type=MESH)

    def greet_seq(s):
        greet(in_seq(target(s)))
        greet(in_seq(source(s)))

    loop(0, 15, greet_seq)
    greet(in_seq(partner))
    def greet_plane(u):
        px, py = lax.rem(x + lax.div(u, 4), 4), lax.rem(y + lax.rem(u, 4), 4)
        greet((px * 2 + zh, py * 8 + zl * 2 + core))
        greet((px * 2 + zh, py * 8 + zl * 2 + 1 - core))

    loop(4, 16, greet_plane)
    loop(0, 4, lambda v: greet((x * 2 + 1 - zh, y * 8 + v * 2 + core)))

    def tile_copy(s, k, dev):
        return remote(
            (pair, cot)[k].at[:, cols(dev), :], recv.at[s, k], tile_s.at[s, k], tile_r.at[s, k], in_seq(dev)
        )

    def send_tile(s):
        dev = target(s)
        tile_copy(s, 0, dev).start()
        tile_copy(s, 1, dev).start()

    row = lax.broadcasted_iota(jnp.int32, (256, 256), 0)
    col = lax.broadcasted_iota(jnp.int32, (256, 256), 1)
    perm[...] = jnp.where(col == (row & 15) * 16 + (row >> 4), 1.0, 0.0).astype(BF16)
    wacc[...] = jnp.zeros_like(wacc)
    accl[...] = jnp.zeros_like(accl)
    accr[...] = jnp.zeros_like(accr)

    def lanes(b):
        return pl.ds(pl.multiple_of(b * 128, 128), 128)

    local[0].wait()
    local[1].wait()

    def tap_parts(b):
        k = taps[:, lanes(b)].astype(F32)
        return k[0:8], k[8:16], k[16:24], k[24:32]

    def pool(b):
        k0, k1, k2, k3 = tap_parts(b)
        for p in range(16):
            t = tokv[p * 16 : p * 16 + 16, lanes(b)].astype(F32)
            lo, hi = t[0:8], t[8:16]
            cen[b, p : p + 1] = jnp.sum(lo * k1 + hi * k2, axis=0, keepdims=True)
            up[b, p + 1 : p + 2] = jnp.sum(hi * k0, axis=0, keepdims=True)
            dn[b, p : p + 1] = jnp.sum(lo * k3, axis=0, keepdims=True)
        halo_out[0, b] = dn[b, 0:1]
        halo_out[1, b] = up[b, 16:17]

    loop(0, NB, pool)
    left, right = lax.rem(me + 31, 32), lax.rem(me + 1, 32)

    def halo(k, j, dev):
        return remote(halo_out.at[k], halo_in.at[k], halo_s.at[k], halo_r.at[k], in_seq(dev))

    def halo_pair(k):
        return halo(k, 0, left), halo(k + 1, 1, right)

    def tok_halo(k, dev):
        rows = pl.ds(240 * k, 16)
        return remote(tokens.at[rows, :], tokh.at[k], th_s.at[k], th_r.at[k], in_seq(dev))

    pl.semaphore_wait(barrier, 59)
    to_left, to_right = halo_pair(0)
    to_left.start()
    to_right.start()
    loop(0, EARLY, send_tile)
    to_left.wait()
    to_right.wait()
    first = jnp.where(me == 0, 0.0, 1.0)
    last = jnp.where(me == 31, 0.0, 1.0)

    def finish_pool(b, total):
        up[b, 0:1] = halo_in[1, b] * first
        dn[b, 16:17] = halo_in[0, b] * last
        v = cen[b] + up[b, 0:16] + dn[b, 1:17]
        cen[b] = v
        return total + v * v

    squares = lax.fori_loop(0, NB, finish_pool, jnp.zeros((16, 128), F32))
    inv = lax.rsqrt(jnp.sum(squares, axis=1, keepdims=True) / (NB * 128.0) + 1e-6)
    for c in local[2:5]:
        c.wait()

    def project(b, total):
        n = (cen[b] * inv * gain[lanes(b)].reshape(1, 128)).astype(BF16)
        normed[b] = n
        return total + dot(n, wcat[pl.ds(pl.multiple_of(b * 128, 128), 128), :], 1, 0)

    feats[me] = lax.fori_loop(0, NB, project, jnp.zeros((16, 256), F32)).astype(BF16)

    def feat_copy(slot, dev):
        return remote(feats.at[me], feats.at[me], feat_s.at[slot], feat_r.at[me], in_seq(dev))

    def feat_arrived(k):
        remote(feats.at[k], feats.at[k], feat_s.at[31], feat_r.at[k], in_seq(k)).wait_recv()

    def send_feat(s):
        feat_copy(s, source(s)).start()
        feat_copy(15 + s, target(s)).start()

    feat_copy(30, partner).start()
    loop(0, 15, send_feat)
    loop(EARLY, 15, send_tile)
    tile_copy(15, 0, partner).start()
    tile_copy(15, 1, partner).start()
    tok_halo(0, left).start()
    tok_halo(1, right).start()

    def n_copy(g):
        return remote(normed.at[lax.rem(g, NB)], nin.at[mine], n_s.at[g], n_r.at[mine], owner(g))

    def arrived(buf, sems, k):
        remote(buf.at[k], buf.at[k], n_s.at[0], sems.at[k], owner(k)).wait_recv()

    def others(lo, hi, f):
        @pl.when(lo < hi)
        def _():
            loop(lo, jnp.clip(mine, lo, hi), f)
            loop(jnp.clip(mine + 1, lo, hi), hi, f)

    others(0, 24, lambda g: n_copy(g).start())

    for c in local[5:]:
        c.wait()

    def add_left_right(grad, f):
        accl[...] += grad * f[:, 128:][None]
        accr[...] += grad * f[:, :128][None]

    def tile(s, k, weight):
        own = jnp.concatenate(
            [pairv[:, cols(k), :].reshape(256, 128), cotv[:, cols(k), :].reshape(256, 128)], axis=1
        )
        other = jnp.concatenate([recv[s, 0].reshape(256, 128), recv[s, 1].reshape(256, 128)], axis=1)
        both = own.astype(F32) + dot(perm[...], other, 1, 0)
        here, theirs = feats[me].astype(F32), feats[k].astype(F32)
        outer = here[:, None, :128] * theirs[None, :, 128:] + here[:, None, 128:] * theirs[None, :, :128]
        sym = (both[:, :128] + outer.reshape(256, 128)).astype(BF16)
        cs = both[:, 128:]
        csb = cs.astype(BF16)
        pre = dot(sym, wa[...], 1, 0)
        sig = 0.5 * jnp.tanh(0.5 * pre) + 0.5
        act = pre * sig
        gpre = (dot(csb, wb[...], 1, 1) * (sig + act * (1.0 - sig))).astype(BF16)
        grad = cs + dot(gpre, wa[...], 1, 1)
        wacc[0] += dot(sym, gpre, 0, 0) * weight
        wacc[1] += dot(csb, act.astype(BF16), 0, 0) * weight
        add_left_right(grad.reshape(16, 16, 128), theirs)
        gradb = grad.astype(BF16)
        gpair[:, cols(k), :] = gradb.reshape(16, 16, 128)
        return gradb

    tile(16, me, 0.5)
    tile_copy(15, 0, partner).wait()
    tile_copy(15, 1, partner).wait()
    feat_arrived(partner)
    tile(15, partner, 0.5)

    def ret_copy(s, dev):
        return remote(rbuf.at[s], gpair.at[:, cols(me), :], ret_s.at[s], ret_r.at[s], in_seq(dev))

    def owned(s):
        k = source(s)
        dev = target(s)
        feat_arrived(k)
        tile_copy(s, 0, dev).wait_recv()
        tile_copy(s, 1, dev).wait_recv()
        gradb = tile(s, k, 1.0)
        rbuf[s] = dot(perm[...], gradb, 1, 0).astype(BF16).reshape(16, 16, 128)
        ret_copy(s, k).start()

    loop(0, 15, owned)

    for q in range(4):
        lane = slice(q * 128, q * 128 + 128)
        w3_out[q] = (wacc[0, :, lane] * scale).reshape(8, 16, 128).astype(BF16)
        w3_out[4 + q] = (wacc[1, :, lane].T * scale).reshape(8, 16, 128).astype(BF16)

    def w3_copy(g):
        return remote(w3_out.at[g - 24], w3_in.at[mine], w3_s.at[g - 24], w3_r.at[mine], owner(g))

    others(24, 32, lambda g: w3_copy(g).start())

    def returned(s):
        k = target(s)
        feat_arrived(k)
        remote(rbuf.at[s], gpair.at[:, cols(k), :], ret_s.at[s], ret_r.at[s], in_seq(k)).wait_recv()
        add_left_right(gpair[:, cols(k), :].astype(F32), feats[k].astype(F32))

    loop(0, 15, returned)
    pair_out = pltpu.make_async_copy(gpair, g_pair, loc.at[11])
    pair_out.start()

    glr_out[0] = jnp.sum(accl[...], axis=1).astype(BF16)
    glr_out[1] = jnp.sum(accr[...], axis=1).astype(BF16)

    def g_copy(g):
        return remote(glr_out.at[lax.div(g, NB)], gin.at[mine], g_s.at[g], g_r.at[mine], owner(g))

    others(0, 24, lambda g: g_copy(g).start())
    glr = jnp.concatenate([glr_out[0], glr_out[1]], axis=1)

    def grad_norm(b, carry):
        total, unused = carry
        gn = dot(glr, wcat[pl.ds(pl.multiple_of(b * 128, 128), 128), :], 1, 1)
        scaled = gn * gain[lanes(b)].reshape(1, 128)
        gpx[b, 1:17] = scaled
        mid[8, pl.ds(b, 1)] = jnp.sum(gn * cen[b] * inv, axis=0, keepdims=True) * scale
        return total + scaled * cen[b], unused

    mid[8] = jnp.zeros((16, 128), F32)
    total, _ = lax.fori_loop(0, NB, grad_norm, (jnp.zeros((16, 128), F32), 0))
    mean = jnp.sum(total, axis=1, keepdims=True) / (NB * 128.0) * inv * inv * inv

    def grad_pool(b):
        v = (gpx[b, 1:17] * inv - cen[b] * mean).astype(BF16).astype(F32)
        gpx[b, 1:17] = v
        halo_out[2, b] = v[0:1]
        halo_out[3, b] = v[15:16]

    loop(0, NB, grad_pool)
    to_left2, to_right2 = halo_pair(2)
    to_left2.start()
    to_right2.start()

    w2_out[24] = mid[8].astype(BF16)
    for g in range(25, 32):
        w2_out[g] = jnp.zeros((16, 128), BF16)
    tok_halo(0, left).wait_recv()
    tok_halo(1, right).wait_recv()

    def taps_grad(b):
        s0 = s1 = s2 = s3 = jnp.zeros((8, 128), F32)
        hi_before = tokh[1, :, lanes(b)].astype(F32)[8:16] * first
        t = tokv[0:16, lanes(b)].astype(F32)
        for p in range(16):
            here = gpx[b, p + 1 : p + 2]
            lo, hi = t[0:8], t[8:16]
            if p < 15:
                t = tokv[p * 16 + 16 : p * 16 + 32, lanes(b)].astype(F32)
                lo_after = t[0:8]
            else:
                lo_after = tokh[0, :, lanes(b)].astype(F32)[0:8] * last
            s0 = s0 + here * hi_before
            s1 = s1 + here * lo
            s2 = s2 + here * hi
            s3 = s3 + here * lo_after
            hi_before = hi
        w2_out[2 * b] = (jnp.concatenate([s0, s1], axis=0) * scale).astype(BF16)
        w2_out[2 * b + 1] = (jnp.concatenate([s2, s3], axis=0) * scale).astype(BF16)

    loop(0, NB, taps_grad)

    def w2_copy(g):
        return remote(w2_out.at[g], w2_in.at[mine], w2_s.at[g], w2_r.at[mine], owner(g))

    others(0, 32, lambda g: w2_copy(g).start())

    @pl.when(mine < 24)
    def _():
        others(0, 32, lambda k: arrived(nin, n_r, k))
        nin[mine] = normed[lax.rem(mine, NB)]
        others(0, 32, lambda k: arrived(gin, g_r, k))
        gin[mine] = glr_out[lax.div(mine, NB)]
        prod = dot(nin[...].reshape(512, 128), gin[...].reshape(512, 128), 0, 0) * scale
        mid[0:8] = prod.reshape(8, 16, 128)

    @pl.when(mine >= 24)
    def _():
        others(0, 32, lambda k: arrived(w3_in, w3_r, k))
        w3_in[mine] = w3_out[jnp.maximum(mine - 24, 0)]
        mid[0:8] = lax.fori_loop(1, 32, lambda k, t: t + w3_in[k].astype(F32), w3_in[0].astype(F32))

    others(0, 32, lambda k: arrived(w2_in, w2_r, k))
    w2_in[mine] = w2_out[mine]
    mid[8] = lax.fori_loop(1, 32, lambda k, t: t + w2_in[k].astype(F32), w2_in[0].astype(F32))

    def c_copy(t, dev, slot):
        return (
            remote(mid.at[t], recv_c.at[slot, 0], c_s.at[t, 0], c_r.at[slot, 0], dev),
            remote(mid.at[8], recv_c.at[slot, 1], c_s.at[t, 1], c_r.at[slot, 1], dev),
        )

    def to_ring(v):
        t, dev = ring(v)
        for c in c_copy(t, dev, zz):
            c.start()

    loop(1, 8, to_ring)
    recv_c[zz, 0] = mid[zz]
    recv_c[zz, 1] = mid[8]

    to_left2.wait()
    to_right2.wait()

    def token_grad(b):
        k0, k1, k2, k3 = tap_parts(b)
        gpx[b, 0:1] = halo_in[3, b] * first
        gpx[b, 17:18] = halo_in[2, b] * last
        for p in range(16):
            before, here, after = gpx[b, p : p + 1], gpx[b, p + 1 : p + 2], gpx[b, p + 2 : p + 3]
            g = jnp.concatenate([here * k1 + before * k3, here * k2 + after * k0], axis=0)
            gtokv[p * 16 : p * 16 + 16, lanes(b)] = g.astype(BF16)

    loop(0, NB, token_grad)
    tok_out = pltpu.make_async_copy(gtokv, g_tokens, loc.at[12])
    tok_out.start()

    def from_ring(v):
        t, dev = ring(v)
        for c in c_copy(t, dev, t):
            c.wait_recv()

    loop(1, 8, from_ring)
    summed = recv_c[0]
    for t in range(1, 8):
        summed = summed + recv_c[t]
    fin[zz] = summed[0].astype(BF16)
    fin[8] = summed[1].astype(BF16)

    def f_copy(slot, v, dev):
        return remote(fin.at[slot], fin.at[slot], f_s.at[v], f_r.at[slot], dev)

    loop(1, 8, lambda v: f_copy(zz, v, ring(v)[1]).start())
    loop(1, 8, lambda v: f_copy(ring(v)[0], v, ring(v)[1]).wait_recv())

    def d_copy(u, dev, g):
        return remote(fin, gat.at[g], d_s.at[u], d_r.at[u], dev)

    loop(1, 16, lambda u: d_copy(u, plane(u)[1], mine).start())
    own = pltpu.make_async_copy(fin, gat.at[mine], loc.at[13])
    own.start()
    own.wait()

    def e_copy(u, g):
        return remote(gat.at[g], gat.at[g], e_s.at[u], e_r.at[u], in_seq(partner))

    e_copy(0, mine).start()

    def back(u):
        px, py = lax.rem(x + 4 - lax.div(u, 4), 4), lax.rem(y + 4 - lax.rem(u, 4), 4)
        return px, py

    def forward(u):
        px, py = back(u)
        g = chunk_of(px, py, core)
        d_copy(u, plane(u)[1], g).wait_recv()
        e_copy(u, g).start()

    loop(1, 16, forward)

    def finish(u):
        px, py = back(u)
        e_copy(u, chunk_of(px, py, 1 - core)).wait_recv()

    loop(0, 16, finish)

    def drain_tile(s):
        dev = target(s)
        tile_copy(s, 0, dev).wait_send()
        tile_copy(s, 1, dev).wait_send()
        feat_copy(s, source(s)).wait_send()
        feat_copy(15 + s, dev).wait_send()
        ret_copy(s, source(s)).wait_send()

    loop(0, 15, drain_tile)
    pair_out.wait()
    tok_out.wait()
    feat_copy(30, partner).wait_send()
    tok_halo(0, left).wait_send()
    tok_halo(1, right).wait_send()

    def drain_features(g):
        n_copy(g).wait_send()
        g_copy(g).wait_send()

    others(0, 24, drain_features)
    others(24, 32, lambda g: w3_copy(g).wait_send())
    others(0, 32, lambda g: w2_copy(g).wait_send())
    loop(1, 16, lambda u: d_copy(u, plane(u)[1], mine).wait_send())

    def drain_forward(u):
        px, py = back(u)
        e_copy(u, chunk_of(px, py, core)).wait_send()

    loop(0, 16, drain_forward)

    def drain_ring(v):
        t, dev = ring(v)
        for c in c_copy(t, dev, zz):
            c.wait_send()
        f_copy(zz, v, dev).wait_send()

    loop(1, 8, drain_ring)


def finish(tok_h, pair_h, gat_h, g_tokens, g_pair, g_lw, g_rw, g_taps, g_gain, g_wa, g_wb, pairv, tokv, gat, lwv, rwv, tapsv, gainv, wav, wbv, sem):
    def put(src, dst, k):
        c = pltpu.make_async_copy(src, dst, sem.at[k])
        c.start()
        return c

    weights = put(gat_h, gat, 8)
    parts = [put(pair_h.at[pl.ds(4 * q, 4)], pairv.at[pl.ds(4 * q, 4)], 9 + q) for q in range(4)]
    toks = put(tok_h, tokv, 13)
    weights.wait()
    copies = []
    for b in range(NB):
        rows = slice(b * 128, b * 128 + 128)
        lwv[rows, :] = gat[b, 0:8].reshape(128, 128).astype(F32)
        rwv[rows, :] = gat[b + 12, 0:8].reshape(128, 128).astype(F32)
    copies += [put(lwv, g_lw, 2), put(rwv, g_rw, 3)]
    for q in range(4):
        lane = slice(q * 128, q * 128 + 128)
        wav[:, lane] = gat[24 + q, 0:8].reshape(128, 128).astype(F32)
        wbv[lane, :] = gat[28 + q, 0:8].reshape(128, 128).astype(F32)
    copies += [put(wav, g_wa, 4), put(wbv, g_wb, 5)]
    gains = gat[24, 8].astype(F32)
    for b in range(NB):
        rows = slice(b * 128, b * 128 + 128)
        tapsv[0:16, rows] = gat[2 * b, 8].astype(F32)
        tapsv[16:32, rows] = gat[2 * b + 1, 8].astype(F32)
        gainv[rows] = gains[b]
    copies += [put(tapsv, g_taps, 6), put(gainv, g_gain, 7)]
    for q in range(4):
        parts[q].wait()
        copies.append(put(pairv.at[pl.ds(4 * q, 4)], g_pair.at[pl.ds(4 * q, 4)], 14 + q))
    toks.wait()
    copies.append(put(tokv, g_tokens, 1))
    for c in copies:
        c.wait()


def local(tokens, pair_in, cotangent, kernel, norm_gain, left_weight, right_weight, transition_a, transition_b):
    plen = pair_in.shape[2]
    scale = 1.0 / math.sqrt(lax.axis_size("dp") * plen * plen)
    hbm = pl.BlockSpec(memory_space=pltpu.HBM)
    dma = pltpu.SemaphoreType.DMA
    tile = (16, 16, 128)
    chunk = (9, 16, 128)
    held = pl.pallas_call(
        functools.partial(body, scale),
        out_shape=(
            jax.ShapeDtypeStruct((256, 1536), BF16),
            jax.ShapeDtypeStruct((16, 512, 128), BF16),
            jax.ShapeDtypeStruct((32,) + chunk, BF16),
        ),
        in_specs=[hbm] * 9,
        out_specs=(hbm,) * 3,
        scratch_shapes=[
            pltpu.VMEM((256, 1536), BF16),
            pltpu.VMEM((16, 512, 128), BF16),
            pltpu.VMEM((256, 1536), BF16),
            pltpu.VMEM((2, 16, 1536), BF16),
            pltpu.VMEM((16, 512, 128), BF16),
            pltpu.VMEM((16, 512, 128), BF16),
            pltpu.VMEM((17, 2) + tile, BF16),
            pltpu.VMEM((15,) + tile, BF16),
            pltpu.VMEM((32, 16, 256), BF16),
            pltpu.VMEM((256, 256), BF16),
            pltpu.VMEM((1536, 256), BF16),
            pltpu.VMEM((32, 1536), BF16),
            pltpu.VMEM((1536,), F32),
            pltpu.VMEM((128, 512), BF16),
            pltpu.VMEM((512, 128), BF16),
            pltpu.VMEM((NB, 16, 128), F32),
            pltpu.VMEM((NB, 24, 128), F32),
            pltpu.VMEM((NB, 24, 128), F32),
            pltpu.VMEM((NB, 16, 128), BF16),
            pltpu.VMEM((NB, 24, 128), F32),
            pltpu.VMEM((4, NB, 1, 128), F32),
            pltpu.VMEM((4, NB, 1, 128), F32),
            pltpu.VMEM(tile, F32),
            pltpu.VMEM(tile, F32),
            pltpu.VMEM((2, 128, 512), F32),
            pltpu.VMEM((2, 16, 128), BF16),
            pltpu.VMEM((32, 16, 128), BF16),
            pltpu.VMEM((32, 16, 128), BF16),
            pltpu.VMEM((8, 8, 16, 128), BF16),
            pltpu.VMEM((32, 8, 16, 128), BF16),
            pltpu.VMEM((32, 16, 128), BF16),
            pltpu.VMEM((32, 16, 128), BF16),
            pltpu.VMEM(chunk, F32),
            pltpu.VMEM((8, 2, 16, 128), F32),
            pltpu.VMEM(chunk, BF16),
            dma((14,)),
            dma((16, 2)),
            dma((16, 2)),
            dma((32,)),
            dma((32,)),
            dma((15,)),
            dma((15,)),
            dma((4,)),
            dma((4,)),
            dma((2,)),
            dma((2,)),
            dma((24,)),
            dma((32,)),
            dma((24,)),
            dma((32,)),
            dma((8,)),
            dma((32,)),
            dma((32,)),
            dma((32,)),
            dma((8, 2)),
            dma((8, 2)),
            dma((8,)),
            dma((8,)),
            dma((16,)),
            dma((16,)),
            dma((16,)),
            dma((16,)),
        ],
        compiler_params=pltpu.CompilerParams(
            collective_id=0, has_side_effects=True, vmem_limit_bytes=VMEM_LIMIT
        ),
    )(
        tokens[0],
        pair_in[0],
        cotangent[0],
        kernel,
        norm_gain,
        left_weight,
        right_weight,
        transition_a,
        transition_b,
    )
    outs = pl.pallas_call(
        finish,
        out_shape=(
            jax.ShapeDtypeStruct((256, 1536), BF16),
            jax.ShapeDtypeStruct((16, 512, 128), BF16),
            jax.ShapeDtypeStruct((1536, 128), F32),
            jax.ShapeDtypeStruct((1536, 128), F32),
            jax.ShapeDtypeStruct((32, 1536), F32),
            jax.ShapeDtypeStruct((1536,), F32),
            jax.ShapeDtypeStruct((128, 512), F32),
            jax.ShapeDtypeStruct((512, 128), F32),
        ),
        in_specs=[hbm] * 3,
        out_specs=(hbm,) * 8,
        scratch_shapes=[
            pltpu.VMEM((16, 512, 128), BF16),
            pltpu.VMEM((256, 1536), BF16),
            pltpu.VMEM((32,) + chunk, BF16),
            pltpu.VMEM((1536, 128), F32),
            pltpu.VMEM((1536, 128), F32),
            pltpu.VMEM((32, 1536), F32),
            pltpu.VMEM((1536,), F32),
            pltpu.VMEM((128, 512), F32),
            pltpu.VMEM((512, 128), F32),
            dma((18,)),
        ],
        compiler_params=pltpu.CompilerParams(vmem_limit_bytes=VMEM_LIMIT),
    )(*held)
    return (outs[0][None], outs[1][None], outs[2], outs[3], outs[4], outs[5], outs[6], outs[7])


def solution(mesh):
    placed = (
        P("dp", "seq", None),
        P("dp", "seq", None, None),
        P("dp", "seq", None, None),
        P(),
        P(),
        P(),
        P(),
        P(),
        P(),
    )
    return jax.shard_map(
        local,
        mesh=mesh,
        in_specs=placed,
        out_specs=(P("dp", "seq", None), P("dp", "seq", None, None), P(), P(), P(), P(), P(), P()),
        check_vma=False,
    )
```

```python
import functools
import math

import jax
import jax.numpy as jnp
from jax import lax
from jax.experimental import pallas as pl
from jax.experimental.pallas import tpu as pltpu
from jax.sharding import PartitionSpec as P

POOL = 16
NB = 12
EARLY = 3
AHEAD = 15
VMEM_LIMIT = 58 * 1024 * 1024
F32 = jnp.float32
BF16 = jnp.bfloat16
MESH = pl.DeviceIdType.MESH


def dot(a, b, ca, cb):
    return lax.dot_general(a, b, (((ca,), (cb,)), ((), ())), preferred_element_type=F32)


def body(
    scale,
    tokens,
    pair,
    cot,
    taps_h,
    gain_h,
    lw,
    rw,
    wa_h,
    wb_h,
    g_tokens,
    g_pair,
    gat,
    gtokv,
    gpair,
    tokv,
    tokh,
    pairv,
    cotv,
    recv,
    rbuf,
    feats,
    perm,
    wcat,
    taps,
    gain,
    wa,
    wb,
    cen,
    up,
    dn,
    normed,
    gpx,
    halo_out,
    halo_in,
    accl,
    accr,
    wacc,
    glr_out,
    nin,
    gin,
    w3_out,
    w3_in,
    w2_out,
    w2_in,
    mid,
    ring_out,
    recv_c,
    fin,
    loc,
    tile_s,
    tile_r,
    feat_s,
    feat_r,
    ret_s,
    ret_r,
    halo_s,
    halo_r,
    th_s,
    th_r,
    n_s,
    n_r,
    g_s,
    g_r,
    w3_s,
    w3_r,
    w2_s,
    w2_r,
    c_s,
    c_r,
    f_s,
    f_r,
    d_s,
    d_r,
    e_s,
    e_r,
):
    dpi = lax.axis_index("dp")
    me = lax.axis_index("seq")
    x, zh = lax.div(dpi, 2), lax.rem(dpi, 2)
    chip, core = lax.div(me, 2), lax.rem(me, 2)
    y, zl = lax.div(chip, 4), lax.rem(chip, 4)
    zz = zh * 4 + zl
    partner = chip * 2 + 1 - core

    def step(s):
        return lax.div(s + 1, 4), lax.rem(s + 1, 4)

    def target(s):
        dy, dz = step(s)
        q = lax.rem(y + dy, 4) * 4 + lax.rem(zl + dz, 4)
        return q * 2 + jnp.where(q > chip, core, 1 - core)

    def source(s):
        dy, dz = step(s)
        r = lax.rem(y + 4 - dy, 4) * 4 + lax.rem(zl + 4 - dz, 4)
        return r * 2 + jnp.where(r < chip, core, 1 - core)

    def in_seq(k):
        return (dpi, k)

    def plane(u):
        px, py = lax.rem(x + lax.div(u, 4), 4), lax.rem(y + lax.rem(u, 4), 4)
        return chunk_of(px, py, core), (px * 2 + zh, py * 8 + zl * 2 + core)

    def chunk_of(px, py, pc):
        odd = lax.rem(px + py, 2)
        return jnp.where(pc == 0, px * 4 + py, 16 + (1 - odd) * 8 + px * 2 + lax.div(py, 2))

    def owner(g):
        t = lax.rem(g, 16)
        e, r = lax.div(t, 8), lax.rem(t, 8)
        rx = lax.div(r, 2)
        ry = lax.rem(r, 2) * 2 + lax.rem(1 - e + rx, 2)
        px = jnp.where(g < 16, lax.div(t, 4), rx)
        py = jnp.where(g < 16, lax.rem(t, 4), ry)
        return (px * 2 + zh, py * 8 + zl * 2 + lax.div(g, 16))

    mine = chunk_of(x, y, core)

    def ring(v):
        t = lax.rem(zz + v, 8)
        return t, (x * 2 + lax.div(t, 4), y * 8 + lax.rem(t, 4) * 2 + core)

    def remote(src, dst, ssem, rsem, dev):
        return pltpu.make_async_remote_copy(
            src_ref=src, dst_ref=dst, send_sem=ssem, recv_sem=rsem, device_id=dev, device_id_type=MESH
        )

    def cols(k):
        return pl.ds(pl.multiple_of(k * 16, 16), 16)

    def fidx(k):
        return lax.rem(k, 2) * 16 + lax.div(k, 2)

    def loop(lo, hi, f):
        def g(i, carry):
            f(i)
            return carry

        lax.fori_loop(lo, hi, g, 0)

    local = [
        pltpu.make_async_copy(tokens, tokv, loc.at[0]),
        pltpu.make_async_copy(taps_h, taps, loc.at[1]),
        pltpu.make_async_copy(gain_h, gain, loc.at[2]),
        pltpu.make_async_copy(lw, wcat.at[:, pl.ds(0, 128)], loc.at[3]),
        pltpu.make_async_copy(rw, wcat.at[:, pl.ds(128, 128)], loc.at[4]),
        pltpu.make_async_copy(wa_h, wa, loc.at[5]),
        pltpu.make_async_copy(wb_h, wb, loc.at[6]),
        pltpu.make_async_copy(pair, pairv, loc.at[7]),
        pltpu.make_async_copy(cot, cotv, loc.at[8]),
        pltpu.make_async_copy(pair.at[:, cols(me), :], recv.at[16, 0], loc.at[9]),
        pltpu.make_async_copy(cot.at[:, cols(me), :], recv.at[16, 1], loc.at[10]),
    ]
    for c in local:
        c.start()

    barrier = pltpu.get_barrier_semaphore()

    def greet(dev):
        pl.semaphore_signal(barrier, inc=1, device_id=dev, device_id_type=MESH)

    def greet_seq(s):
        greet(in_seq(target(s)))
        greet(in_seq(source(s)))

    loop(0, 15, greet_seq)
    greet(in_seq(partner))
    def greet_plane(u):
        px, py = lax.rem(x + lax.div(u, 4), 4), lax.rem(y + lax.rem(u, 4), 4)
        greet((px * 2 + zh, py * 8 + zl * 2 + core))
        greet((px * 2 + zh, py * 8 + zl * 2 + 1 - core))

    loop(4, 16, greet_plane)
    loop(0, 4, lambda v: greet((x * 2 + 1 - zh, y * 8 + v * 2 + core)))

    def tile_copy(s, k, dev):
        return remote(
            (pair, cot)[k].at[:, cols(dev), :], recv.at[s, k], tile_s.at[s, k], tile_r.at[s, k], in_seq(dev)
        )

    def send_tile(s):
        dev = target(s)
        tile_copy(s, 0, dev).start()
        tile_copy(s, 1, dev).start()

    row = lax.broadcasted_iota(jnp.int32, (256, 256), 0)
    col = lax.broadcasted_iota(jnp.int32, (256, 256), 1)
    perm[...] = jnp.where(col == (row & 15) * 16 + (row >> 4), 1.0, 0.0).astype(BF16)
    wacc[...] = jnp.zeros_like(wacc)
    accl[...] = jnp.zeros_like(accl)
    accr[...] = jnp.zeros_like(accr)

    def lanes(b):
        return pl.ds(pl.multiple_of(b * 128, 128), 128)

    local[0].wait()
    local[1].wait()

    def tap_parts(b):
        k = taps[:, lanes(b)].astype(F32)
        return k[0:8], k[8:16], k[16:24], k[24:32]

    def pool(b):
        k0, k1, k2, k3 = tap_parts(b)
        for p in range(16):
            t = tokv[p * 16 : p * 16 + 16, lanes(b)].astype(F32)
            lo, hi = t[0:8], t[8:16]
            cen[b, p : p + 1] = jnp.sum(lo * k1 + hi * k2, axis=0, keepdims=True)
            up[b, p + 1 : p + 2] = jnp.sum(hi * k0, axis=0, keepdims=True)
            dn[b, p : p + 1] = jnp.sum(lo * k3, axis=0, keepdims=True)
        halo_out[0, b] = dn[b, 0:1]
        halo_out[1, b] = up[b, 16:17]

    loop(0, NB, pool)
    left, right = lax.rem(me + 31, 32), lax.rem(me + 1, 32)

    def halo(k, j, dev):
        return remote(halo_out.at[k], halo_in.at[k], halo_s.at[k], halo_r.at[k], in_seq(dev))

    def halo_pair(k):
        return halo(k, 0, left), halo(k + 1, 1, right)

    def tok_halo(k, dev):
        rows = pl.ds(240 * k, 16)
        return remote(tokens.at[rows, :], tokh.at[k], th_s.at[k], th_r.at[k], in_seq(dev))

    pl.semaphore_wait(barrier, 59)
    to_left, to_right = halo_pair(0)
    to_left.start()
    to_right.start()
    loop(0, EARLY, send_tile)
    to_left.wait()
    to_right.wait()
    first = jnp.where(me == 0, 0.0, 1.0)
    last = jnp.where(me == 31, 0.0, 1.0)

    def finish_pool(b, total):
        up[b, 0:1] = halo_in[1, b] * first
        dn[b, 16:17] = halo_in[0, b] * last
        v = cen[b] + up[b, 0:16] + dn[b, 1:17]
        cen[b] = v
        return total + v * v

    squares = lax.fori_loop(0, NB, finish_pool, jnp.zeros((16, 128), F32))
    inv = lax.rsqrt(jnp.sum(squares, axis=1, keepdims=True) / (NB * 128.0) + 1e-6)
    for c in local[2:5]:
        c.wait()

    def project(b, total):
        n = (cen[b] * inv * gain[lanes(b)].reshape(1, 128)).astype(BF16)
        normed[b] = n
        return total + dot(n, wcat[pl.ds(pl.multiple_of(b * 128, 128), 128), :], 1, 0)

    feats[fidx(me)] = lax.fori_loop(0, NB, project, jnp.zeros((16, 256), F32)).astype(BF16)

    def hop1(v):
        block = feats.at[fidx(me)]
        return remote(block, block, feat_s.at[v], feat_r.at[v], in_seq(y * 8 + lax.rem(zl + v, 4) * 2 + core))

    def hop2(v):
        block = feats.at[pl.ds(core * 16 + y * 4, 4)]
        return remote(block, block, feat_s.at[3 + v], feat_r.at[3 + v], in_seq(lax.rem(y + v, 4) * 8 + zl * 2 + core))

    def hop3(half):
        block = feats.at[pl.ds(half * 16, 16)]
        return remote(block, block, feat_s.at[0], feat_r.at[0], in_seq(partner))

    for v in (1, 2, 3):
        hop1(v).start()
    loop(EARLY, AHEAD, send_tile)
    tile_copy(15, 0, partner).start()
    tile_copy(15, 1, partner).start()
    tok_halo(0, left).start()
    tok_halo(1, right).start()

    def n_copy(g):
        return remote(normed.at[lax.rem(g, NB)], nin.at[mine], n_s.at[g], n_r.at[mine], owner(g))

    def arrived(buf, sems, k):
        remote(buf.at[k], buf.at[k], n_s.at[0], sems.at[k], owner(k)).wait_recv()

    def others(lo, hi, f):
        @pl.when(lo < hi)
        def _():
            loop(lo, jnp.clip(mine, lo, hi), f)
            loop(jnp.clip(mine + 1, lo, hi), hi, f)

    others(0, 24, lambda g: n_copy(g).start())
    for v in (1, 2, 3):
        hop1(v).wait_recv()
    for v in (1, 2, 3):
        hop2(v).start()

    for c in local[5:]:
        c.wait()

    def add_left_right(grad, f):
        accl[...] += grad * f[:, 128:][None]
        accr[...] += grad * f[:, :128][None]

    def tile(s, k, weight):
        own = jnp.concatenate(
            [pairv[:, cols(k), :].reshape(256, 128), cotv[:, cols(k), :].reshape(256, 128)], axis=1
        )
        other = jnp.concatenate([recv[s, 0].reshape(256, 128), recv[s, 1].reshape(256, 128)], axis=1)
        both = own.astype(F32) + dot(perm[...], other, 1, 0)
        here, theirs = feats[fidx(me)].astype(F32), feats[fidx(k)].astype(F32)
        outer = here[:, None, :128] * theirs[None, :, 128:] + here[:, None, 128:] * theirs[None, :, :128]
        sym = (both[:, :128] + outer.reshape(256, 128)).astype(BF16)
        cs = both[:, 128:]
        csb = cs.astype(BF16)
        pre = dot(sym, wa[...], 1, 0)
        sig = 0.5 * jnp.tanh(0.5 * pre) + 0.5
        act = pre * sig
        gpre = (dot(csb, wb[...], 1, 1) * (sig + act * (1.0 - sig))).astype(BF16)
        grad = cs + dot(gpre, wa[...], 1, 1)
        wacc[0] += dot(sym, gpre, 0, 0) * weight
        wacc[1] += dot(csb, act.astype(BF16), 0, 0) * weight
        add_left_right(grad.reshape(16, 16, 128), theirs)
        gradb = grad.astype(BF16)
        gpair[:, cols(k), :] = gradb.reshape(16, 16, 128)
        return gradb

    tile(16, me, 0.5)
    for v in (1, 2, 3):
        hop2(v).wait_recv()
    hop3(core).start()
    tile_copy(15, 0, partner).wait()
    tile_copy(15, 1, partner).wait()
    hop3(1 - core).wait_recv()
    tile(15, partner, 0.5)

    def ret_copy(s, dev):
        return remote(rbuf.at[s], gpair.at[:, cols(me), :], ret_s.at[s], ret_r.at[s], in_seq(dev))

    def owned(s):
        pl.when(s + AHEAD < 15)(lambda: send_tile(s + AHEAD))
        k = source(s)
        dev = target(s)
        tile_copy(s, 0, dev).wait_recv()
        tile_copy(s, 1, dev).wait_recv()
        gradb = tile(s, k, 1.0)
        rbuf[s] = dot(perm[...], gradb, 1, 0).astype(BF16).reshape(16, 16, 128)
        ret_copy(s, k).start()

    loop(0, 15, owned)

    for q in range(4):
        lane = slice(q * 128, q * 128 + 128)
        w3_out[q] = (wacc[0, :, lane] * scale).reshape(8, 16, 128).astype(BF16)
        w3_out[4 + q] = (wacc[1, :, lane].T * scale).reshape(8, 16, 128).astype(BF16)

    def w3_copy(g):
        return remote(w3_out.at[g - 24], w3_in.at[mine], w3_s.at[g - 24], w3_r.at[mine], owner(g))

    others(24, 32, lambda g: w3_copy(g).start())

    def returned(s):
        k = target(s)
        remote(rbuf.at[s], gpair.at[:, cols(k), :], ret_s.at[s], ret_r.at[s], in_seq(k)).wait_recv()
        add_left_right(gpair[:, cols(k), :].astype(F32), feats[fidx(k)].astype(F32))

    loop(0, 15, returned)
    pair_out = pltpu.make_async_copy(gpair, g_pair, loc.at[11])
    pair_out.start()

    glr_out[0] = jnp.sum(accl[...], axis=1).astype(BF16)
    glr_out[1] = jnp.sum(accr[...], axis=1).astype(BF16)

    def g_copy(g):
        return remote(glr_out.at[lax.div(g, NB)], gin.at[mine], g_s.at[g], g_r.at[mine], owner(g))

    others(0, 24, lambda g: g_copy(g).start())
    glr = jnp.concatenate([glr_out[0], glr_out[1]], axis=1)

    def grad_norm(b, carry):
        total, unused = carry
        gn = dot(glr, wcat[pl.ds(pl.multiple_of(b * 128, 128), 128), :], 1, 1)
        scaled = gn * gain[lanes(b)].reshape(1, 128)
        gpx[b, 1:17] = scaled
        mid[8, pl.ds(b, 1)] = jnp.sum(gn * cen[b] * inv, axis=0, keepdims=True) * scale
        return total + scaled * cen[b], unused

    mid[8] = jnp.zeros((16, 128), F32)
    total, _ = lax.fori_loop(0, NB, grad_norm, (jnp.zeros((16, 128), F32), 0))
    mean = jnp.sum(total, axis=1, keepdims=True) / (NB * 128.0) * inv * inv * inv

    def grad_pool(b):
        v = (gpx[b, 1:17] * inv - cen[b] * mean).astype(BF16).astype(F32)
        gpx[b, 1:17] = v
        halo_out[2, b] = v[0:1]
        halo_out[3, b] = v[15:16]

    loop(0, NB, grad_pool)
    to_left2, to_right2 = halo_pair(2)
    to_left2.start()
    to_right2.start()

    w2_out[24] = mid[8].astype(BF16)
    for g in range(25, 32):
        w2_out[g] = jnp.zeros((16, 128), BF16)
    tok_halo(0, left).wait_recv()
    tok_halo(1, right).wait_recv()

    def taps_grad(b):
        s0 = s1 = s2 = s3 = jnp.zeros((8, 128), F32)
        hi_before = tokh[1, :, lanes(b)].astype(F32)[8:16] * first
        t = tokv[0:16, lanes(b)].astype(F32)
        for p in range(16):
            here = gpx[b, p + 1 : p + 2]
            lo, hi = t[0:8], t[8:16]
            if p < 15:
                t = tokv[p * 16 + 16 : p * 16 + 32, lanes(b)].astype(F32)
                lo_after = t[0:8]
            else:
                lo_after = tokh[0, :, lanes(b)].astype(F32)[0:8] * last
            s0 = s0 + here * hi_before
            s1 = s1 + here * lo
            s2 = s2 + here * hi
            s3 = s3 + here * lo_after
            hi_before = hi
        w2_out[2 * b] = (jnp.concatenate([s0, s1], axis=0) * scale).astype(BF16)
        w2_out[2 * b + 1] = (jnp.concatenate([s2, s3], axis=0) * scale).astype(BF16)

    loop(0, NB, taps_grad)

    def w2_copy(g):
        return remote(w2_out.at[g], w2_in.at[mine], w2_s.at[g], w2_r.at[mine], owner(g))

    others(0, 32, lambda g: w2_copy(g).start())

    @pl.when(mine < 24)
    def _():
        others(0, 32, lambda k: arrived(nin, n_r, k))
        nin[mine] = normed[lax.rem(mine, NB)]
        others(0, 32, lambda k: arrived(gin, g_r, k))
        gin[mine] = glr_out[lax.div(mine, NB)]
        prod = dot(nin[...].reshape(512, 128), gin[...].reshape(512, 128), 0, 0) * scale
        mid[0:8] = prod.reshape(8, 16, 128)

    @pl.when(mine >= 24)
    def _():
        others(0, 32, lambda k: arrived(w3_in, w3_r, k))
        w3_in[mine] = w3_out[jnp.maximum(mine - 24, 0)]
        mid[0:8] = lax.fori_loop(1, 32, lambda k, t: t + w3_in[k].astype(F32), w3_in[0].astype(F32))

    def c_copy(t, dev, slot):
        return remote(ring_out.at[t], recv_c.at[slot, 0], c_s.at[t, 0], c_r.at[slot, 0], dev)

    def c2_copy(t, dev, slot):
        return remote(ring_out.at[8], recv_c.at[slot, 1], c_s.at[t, 1], c_r.at[slot, 1], dev)

    def f_copy(slot, v, dev):
        return remote(fin.at[slot], fin.at[slot], f_s.at[v], f_r.at[slot], dev)

    def on_ring(f):
        loop(1, 8, lambda v: f(v, *ring(v)))

    ring_out[0:8] = mid[0:8].astype(BF16)
    on_ring(lambda v, t, dev: c_copy(t, dev, zz).start())
    recv_c[zz, 0] = ring_out[zz]

    others(0, 32, lambda k: arrived(w2_in, w2_r, k))
    w2_in[mine] = w2_out[mine]
    summed = lax.fori_loop(1, 32, lambda k, t: t + w2_in[k].astype(F32), w2_in[0].astype(F32))
    ring_out[8] = summed.astype(BF16)
    on_ring(lambda v, t, dev: c2_copy(t, dev, zz).start())
    recv_c[zz, 1] = ring_out[8]

    def ring_sum(k):
        return lax.fori_loop(1, 8, lambda t, a: a + recv_c[t, k].astype(F32), recv_c[0, k].astype(F32))

    on_ring(lambda v, t, dev: c_copy(t, dev, t).wait_recv())
    fin[zz] = ring_sum(0).astype(BF16)
    on_ring(lambda v, t, dev: f_copy(zz, v, dev).start())
    on_ring(lambda v, t, dev: c2_copy(t, dev, t).wait_recv())
    fin[8] = ring_sum(1).astype(BF16)
    on_ring(lambda v, t, dev: f_copy(t, v, dev).wait_recv())

    def d_copy(u, dev, g):
        return remote(fin, gat.at[g], d_s.at[u], d_r.at[u], dev)

    loop(1, 16, lambda u: d_copy(u, plane(u)[1], mine).start())
    own = pltpu.make_async_copy(fin, gat.at[mine], loc.at[13])
    own.start()
    own.wait()

    def e_copy(u, g):
        return remote(gat.at[g], gat.at[g], e_s.at[u], e_r.at[u], in_seq(partner))

    e_copy(0, mine).start()
    to_left2.wait()
    to_right2.wait()

    def token_grad(b):
        k0, k1, k2, k3 = tap_parts(b)
        gpx[b, 0:1] = halo_in[3, b] * first
        gpx[b, 17:18] = halo_in[2, b] * last
        for p in range(16):
            before, here, after = gpx[b, p : p + 1], gpx[b, p + 1 : p + 2], gpx[b, p + 2 : p + 3]
            g = jnp.concatenate([here * k1 + before * k3, here * k2 + after * k0], axis=0)
            gtokv[p * 16 : p * 16 + 16, lanes(b)] = g.astype(BF16)

    loop(0, NB, token_grad)
    tok_out = pltpu.make_async_copy(gtokv, g_tokens, loc.at[12])
    tok_out.start()

    def back(u):
        px, py = lax.rem(x + 4 - lax.div(u, 4), 4), lax.rem(y + 4 - lax.rem(u, 4), 4)
        return px, py

    def forward(u):
        px, py = back(u)
        g = chunk_of(px, py, core)
        d_copy(u, plane(u)[1], g).wait_recv()
        e_copy(u, g).start()

    loop(1, 16, forward)

    def finish(u):
        px, py = back(u)
        e_copy(u, chunk_of(px, py, 1 - core)).wait_recv()

    loop(0, 16, finish)

    def drain_tile(s):
        dev = target(s)
        tile_copy(s, 0, dev).wait_send()
        tile_copy(s, 1, dev).wait_send()
        ret_copy(s, source(s)).wait_send()

    loop(0, 15, drain_tile)
    pair_out.wait()
    tok_out.wait()
    for v in (1, 2, 3):
        hop1(v).wait_send()
        hop2(v).wait_send()
    hop3(core).wait_send()
    tok_halo(0, left).wait_send()
    tok_halo(1, right).wait_send()

    def drain_features(g):
        n_copy(g).wait_send()
        g_copy(g).wait_send()

    others(0, 24, drain_features)
    others(24, 32, lambda g: w3_copy(g).wait_send())
    others(0, 32, lambda g: w2_copy(g).wait_send())
    loop(1, 16, lambda u: d_copy(u, plane(u)[1], mine).wait_send())

    def drain_forward(u):
        px, py = back(u)
        e_copy(u, chunk_of(px, py, core)).wait_send()

    loop(0, 16, drain_forward)

    def drain_ring(v, t, dev):
        c_copy(t, dev, zz).wait_send()
        c2_copy(t, dev, zz).wait_send()
        f_copy(zz, v, dev).wait_send()

    on_ring(drain_ring)


def finish(tok_h, pair_h, gat_h, g_tokens, g_pair, g_lw, g_rw, g_taps, g_gain, g_wa, g_wb, pairv, tokv, gat, lwv, rwv, tapsv, gainv, wav, wbv, sem):
    def put(src, dst, k):
        c = pltpu.make_async_copy(src, dst, sem.at[k])
        c.start()
        return c

    weights = put(gat_h, gat, 8)
    parts = [put(pair_h.at[pl.ds(4 * q, 4)], pairv.at[pl.ds(4 * q, 4)], 9 + q) for q in range(4)]
    toks = put(tok_h, tokv, 13)
    weights.wait()
    copies = []
    for b in range(NB):
        rows = slice(b * 128, b * 128 + 128)
        lwv[rows, :] = gat[b, 0:8].reshape(128, 128).astype(F32)
        rwv[rows, :] = gat[b + 12, 0:8].reshape(128, 128).astype(F32)
    copies += [put(lwv, g_lw, 2), put(rwv, g_rw, 3)]
    for q in range(4):
        lane = slice(q * 128, q * 128 + 128)
        wav[:, lane] = gat[24 + q, 0:8].reshape(128, 128).astype(F32)
        wbv[lane, :] = gat[28 + q, 0:8].reshape(128, 128).astype(F32)
    copies += [put(wav, g_wa, 4), put(wbv, g_wb, 5)]
    gains = gat[24, 8].astype(F32)
    for b in range(NB):
        rows = slice(b * 128, b * 128 + 128)
        tapsv[0:16, rows] = gat[2 * b, 8].astype(F32)
        tapsv[16:32, rows] = gat[2 * b + 1, 8].astype(F32)
        gainv[rows] = gains[b]
    copies += [put(tapsv, g_taps, 6), put(gainv, g_gain, 7)]
    for q in range(4):
        parts[q].wait()
        copies.append(put(pairv.at[pl.ds(4 * q, 4)], g_pair.at[pl.ds(4 * q, 4)], 14 + q))
    toks.wait()
    copies.append(put(tokv, g_tokens, 1))
    for c in copies:
        c.wait()


def local(tokens, pair_in, cotangent, kernel, norm_gain, left_weight, right_weight, transition_a, transition_b):
    plen = pair_in.shape[2]
    scale = 1.0 / math.sqrt(lax.axis_size("dp") * plen * plen)
    hbm = pl.BlockSpec(memory_space=pltpu.HBM)
    dma = pltpu.SemaphoreType.DMA
    tile = (16, 16, 128)
    chunk = (9, 16, 128)
    held = pl.pallas_call(
        functools.partial(body, scale),
        out_shape=(
            jax.ShapeDtypeStruct((256, 1536), BF16),
            jax.ShapeDtypeStruct((16, 512, 128), BF16),
            jax.ShapeDtypeStruct((32,) + chunk, BF16),
        ),
        in_specs=[hbm] * 9,
        out_specs=(hbm,) * 3,
        scratch_shapes=[
            pltpu.VMEM((256, 1536), BF16),
            pltpu.VMEM((16, 512, 128), BF16),
            pltpu.VMEM((256, 1536), BF16),
            pltpu.VMEM((2, 16, 1536), BF16),
            pltpu.VMEM((16, 512, 128), BF16),
            pltpu.VMEM((16, 512, 128), BF16),
            pltpu.VMEM((17, 2) + tile, BF16),
            pltpu.VMEM((15,) + tile, BF16),
            pltpu.VMEM((32, 16, 256), BF16),
            pltpu.VMEM((256, 256), BF16),
            pltpu.VMEM((1536, 256), BF16),
            pltpu.VMEM((32, 1536), BF16),
            pltpu.VMEM((1536,), F32),
            pltpu.VMEM((128, 512), BF16),
            pltpu.VMEM((512, 128), BF16),
            pltpu.VMEM((NB, 16, 128), F32),
            pltpu.VMEM((NB, 24, 128), F32),
            pltpu.VMEM((NB, 24, 128), F32),
            pltpu.VMEM((NB, 16, 128), BF16),
            pltpu.VMEM((NB, 24, 128), F32),
            pltpu.VMEM((4, NB, 1, 128), F32),
            pltpu.VMEM((4, NB, 1, 128), F32),
            pltpu.VMEM(tile, F32),
            pltpu.VMEM(tile, F32),
            pltpu.VMEM((2, 128, 512), F32),
            pltpu.VMEM((2, 16, 128), BF16),
            pltpu.VMEM((32, 16, 128), BF16),
            pltpu.VMEM((32, 16, 128), BF16),
            pltpu.VMEM((8, 8, 16, 128), BF16),
            pltpu.VMEM((32, 8, 16, 128), BF16),
            pltpu.VMEM((32, 16, 128), BF16),
            pltpu.VMEM((32, 16, 128), BF16),
            pltpu.VMEM(chunk, F32),
            pltpu.VMEM(chunk, BF16),
            pltpu.VMEM((8, 2, 16, 128), BF16),
            pltpu.VMEM(chunk, BF16),
            dma((14,)),
            dma((16, 2)),
            dma((16, 2)),
            dma((7,)),
            dma((7,)),
            dma((15,)),
            dma((15,)),
            dma((4,)),
            dma((4,)),
            dma((2,)),
            dma((2,)),
            dma((24,)),
            dma((32,)),
            dma((24,)),
            dma((32,)),
            dma((8,)),
            dma((32,)),
            dma((32,)),
            dma((32,)),
            dma((8, 2)),
            dma((8, 2)),
            dma((8,)),
            dma((8,)),
            dma((16,)),
            dma((16,)),
            dma((16,)),
            dma((16,)),
        ],
        compiler_params=pltpu.CompilerParams(
            collective_id=0, has_side_effects=True, vmem_limit_bytes=VMEM_LIMIT
        ),
    )(
        tokens[0],
        pair_in[0],
        cotangent[0],
        kernel,
        norm_gain,
        left_weight,
        right_weight,
        transition_a,
        transition_b,
    )
    outs = pl.pallas_call(
        finish,
        out_shape=(
            jax.ShapeDtypeStruct((256, 1536), BF16),
            jax.ShapeDtypeStruct((16, 512, 128), BF16),
            jax.ShapeDtypeStruct((1536, 128), F32),
            jax.ShapeDtypeStruct((1536, 128), F32),
            jax.ShapeDtypeStruct((32, 1536), F32),
            jax.ShapeDtypeStruct((1536,), F32),
            jax.ShapeDtypeStruct((128, 512), F32),
            jax.ShapeDtypeStruct((512, 128), F32),
        ),
        in_specs=[hbm] * 3,
        out_specs=(hbm,) * 8,
        scratch_shapes=[
            pltpu.VMEM((16, 512, 128), BF16),
            pltpu.VMEM((256, 1536), BF16),
            pltpu.VMEM((32,) + chunk, BF16),
            pltpu.VMEM((1536, 128), F32),
            pltpu.VMEM((1536, 128), F32),
            pltpu.VMEM((32, 1536), F32),
            pltpu.VMEM((1536,), F32),
            pltpu.VMEM((128, 512), F32),
            pltpu.VMEM((512, 128), F32),
            dma((18,)),
        ],
        compiler_params=pltpu.CompilerParams(vmem_limit_bytes=VMEM_LIMIT),
    )(*held)
    return (outs[0][None], outs[1][None], outs[2], outs[3], outs[4], outs[5], outs[6], outs[7])


def solution(mesh):
    placed = (
        P("dp", "seq", None),
        P("dp", "seq", None, None),
        P("dp", "seq", None, None),
        P(),
        P(),
        P(),
        P(),
        P(),
        P(),
    )
    return jax.shard_map(
        local,
        mesh=mesh,
        in_specs=placed,
        out_specs=(P("dp", "seq", None), P("dp", "seq", None, None), P(), P(), P(), P(), P(), P()),
        check_vma=False,
    )
```

```python
import functools
import math

import jax
import jax.numpy as jnp
from jax import lax
from jax.experimental import pallas as pl
from jax.experimental.pallas import tpu as pltpu
from jax.sharding import PartitionSpec as P

POOL = 16
NB = 12
EARLY = 7
AHEAD = 15
VMEM_LIMIT = 58 * 1024 * 1024
F32 = jnp.float32
BF16 = jnp.bfloat16
MESH = pl.DeviceIdType.MESH


def dot(a, b, ca, cb):
    return lax.dot_general(a, b, (((ca,), (cb,)), ((), ())), preferred_element_type=F32)


def body(
    scale,
    tokens,
    pair,
    cot,
    taps_h,
    gain_h,
    lw,
    rw,
    wa_h,
    wb_h,
    g_tokens,
    g_pair,
    gat,
    gtokv,
    gpair,
    tokv,
    tokh,
    pairv,
    cotv,
    recv,
    rbuf,
    feats,
    perm,
    wcat,
    taps,
    gain,
    wa,
    wb,
    cen,
    up,
    dn,
    normed,
    gpx,
    halo_out,
    halo_in,
    accl,
    accr,
    wacc,
    glr_out,
    nin,
    gin,
    w3_out,
    w3_in,
    w2_out,
    w2_in,
    mid,
    ring_out,
    recv_c,
    fin,
    loc,
    tile_s,
    tile_r,
    feat_s,
    feat_r,
    ret_s,
    ret_r,
    halo_s,
    halo_r,
    th_s,
    th_r,
    n_s,
    n_r,
    g_s,
    g_r,
    w3_s,
    w3_r,
    w2_s,
    w2_r,
    c_s,
    c_r,
    f_s,
    f_r,
    d_s,
    d_r,
    e_s,
    e_r,
):
    dpi = lax.axis_index("dp")
    me = lax.axis_index("seq")
    x, zh = lax.div(dpi, 2), lax.rem(dpi, 2)
    chip, core = lax.div(me, 2), lax.rem(me, 2)
    y, zl = lax.div(chip, 4), lax.rem(chip, 4)
    zz = zh * 4 + zl
    partner = chip * 2 + 1 - core

    def step(s):
        return lax.div(15 - s, 4), lax.rem(15 - s, 4)

    def target(s):
        dy, dz = step(s)
        q = lax.rem(y + dy, 4) * 4 + lax.rem(zl + dz, 4)
        return q * 2 + jnp.where(q > chip, core, 1 - core)

    def source(s):
        dy, dz = step(s)
        r = lax.rem(y + 4 - dy, 4) * 4 + lax.rem(zl + 4 - dz, 4)
        return r * 2 + jnp.where(r < chip, core, 1 - core)

    def in_seq(k):
        return (dpi, k)

    def plane(u):
        px, py = lax.rem(x + lax.div(u, 4), 4), lax.rem(y + lax.rem(u, 4), 4)
        return chunk_of(px, py, core), (px * 2 + zh, py * 8 + zl * 2 + core)

    def chunk_of(px, py, pc):
        odd = lax.rem(px + py, 2)
        return jnp.where(pc == 0, px * 4 + py, 16 + (1 - odd) * 8 + px * 2 + lax.div(py, 2))

    def owner(g):
        t = lax.rem(g, 16)
        e, r = lax.div(t, 8), lax.rem(t, 8)
        rx = lax.div(r, 2)
        ry = lax.rem(r, 2) * 2 + lax.rem(1 - e + rx, 2)
        px = jnp.where(g < 16, lax.div(t, 4), rx)
        py = jnp.where(g < 16, lax.rem(t, 4), ry)
        return (px * 2 + zh, py * 8 + zl * 2 + lax.div(g, 16))

    mine = chunk_of(x, y, core)

    def ring(v):
        t = lax.rem(zz + v, 8)
        return t, (x * 2 + lax.div(t, 4), y * 8 + lax.rem(t, 4) * 2 + core)

    def remote(src, dst, ssem, rsem, dev):
        return pltpu.make_async_remote_copy(
            src_ref=src, dst_ref=dst, send_sem=ssem, recv_sem=rsem, device_id=dev, device_id_type=MESH
        )

    def cols(k):
        return pl.ds(pl.multiple_of(k * 16, 16), 16)

    def fidx(k):
        return lax.rem(k, 2) * 16 + lax.div(k, 2)

    def loop(lo, hi, f):
        def g(i, carry):
            f(i)
            return carry

        lax.fori_loop(lo, hi, g, 0)

    local = [
        pltpu.make_async_copy(tokens, tokv, loc.at[0]),
        pltpu.make_async_copy(taps_h, taps, loc.at[1]),
        pltpu.make_async_copy(gain_h, gain, loc.at[2]),
        pltpu.make_async_copy(lw, wcat.at[:, pl.ds(0, 128)], loc.at[3]),
        pltpu.make_async_copy(rw, wcat.at[:, pl.ds(128, 128)], loc.at[4]),
        pltpu.make_async_copy(wa_h, wa, loc.at[5]),
        pltpu.make_async_copy(wb_h, wb, loc.at[6]),
        pltpu.make_async_copy(pair, pairv, loc.at[7]),
        pltpu.make_async_copy(cot, cotv, loc.at[8]),
        pltpu.make_async_copy(pair.at[:, cols(me), :], recv.at[16, 0], loc.at[9]),
        pltpu.make_async_copy(cot.at[:, cols(me), :], recv.at[16, 1], loc.at[10]),
    ]
    for c in local:
        c.start()

    barrier = pltpu.get_barrier_semaphore()

    def greet(dev):
        pl.semaphore_signal(barrier, inc=1, device_id=dev, device_id_type=MESH)

    def greet_seq(s):
        greet(in_seq(target(s)))
        greet(in_seq(source(s)))

    loop(0, 15, greet_seq)
    greet(in_seq(partner))
    def greet_plane(u):
        px, py = lax.rem(x + lax.div(u, 4), 4), lax.rem(y + lax.rem(u, 4), 4)
        greet((px * 2 + zh, py * 8 + zl * 2 + core))
        greet((px * 2 + zh, py * 8 + zl * 2 + 1 - core))

    loop(4, 16, greet_plane)
    loop(0, 4, lambda v: greet((x * 2 + 1 - zh, y * 8 + v * 2 + core)))

    def tile_copy(s, k, dev):
        return remote(
            (pair, cot)[k].at[:, cols(dev), :], recv.at[s, k], tile_s.at[s, k], tile_r.at[s, k], in_seq(dev)
        )

    def send_tile(i):
        s = jnp.where((core == 1) & (i < 14), i + 1 - 2 * lax.rem(i, 2), i)
        dev = target(s)
        tile_copy(s, 0, dev).start()
        tile_copy(s, 1, dev).start()

    row = lax.broadcasted_iota(jnp.int32, (256, 256), 0)
    col = lax.broadcasted_iota(jnp.int32, (256, 256), 1)
    perm[...] = jnp.where(col == (row & 15) * 16 + (row >> 4), 1.0, 0.0).astype(BF16)
    wacc[...] = jnp.zeros_like(wacc)
    accl[...] = jnp.zeros_like(accl)
    accr[...] = jnp.zeros_like(accr)

    def lanes(b):
        return pl.ds(pl.multiple_of(b * 128, 128), 128)

    local[0].wait()
    local[1].wait()

    def tap_parts(b):
        k = taps[:, lanes(b)].astype(F32)
        return k[0:8], k[8:16], k[16:24], k[24:32]

    def pool(b):
        k0, k1, k2, k3 = tap_parts(b)
        for p in range(16):
            t = tokv[p * 16 : p * 16 + 16, lanes(b)].astype(F32)
            lo, hi = t[0:8], t[8:16]
            cen[b, p : p + 1] = jnp.sum(lo * k1 + hi * k2, axis=0, keepdims=True)
            up[b, p + 1 : p + 2] = jnp.sum(hi * k0, axis=0, keepdims=True)
            dn[b, p : p + 1] = jnp.sum(lo * k3, axis=0, keepdims=True)
        halo_out[0, b] = dn[b, 0:1]
        halo_out[1, b] = up[b, 16:17]

    loop(0, NB, pool)
    left, right = lax.rem(me + 31, 32), lax.rem(me + 1, 32)

    def halo(k, j, dev):
        return remote(halo_out.at[k], halo_in.at[k], halo_s.at[k], halo_r.at[k], in_seq(dev))

    def halo_pair(k):
        return halo(k, 0, left), halo(k + 1, 1, right)

    def tok_halo(k, dev):
        rows = pl.ds(240 * k, 16)
        return remote(tokens.at[rows, :], tokh.at[k], th_s.at[k], th_r.at[k], in_seq(dev))

    pl.semaphore_wait(barrier, 59)
    to_left, to_right = halo_pair(0)
    to_left.start()
    to_right.start()
    loop(0, EARLY, send_tile)
    to_left.wait()
    to_right.wait()
    first = jnp.where(me == 0, 0.0, 1.0)
    last = jnp.where(me == 31, 0.0, 1.0)

    def finish_pool(b, total):
        up[b, 0:1] = halo_in[1, b] * first
        dn[b, 16:17] = halo_in[0, b] * last
        v = cen[b] + up[b, 0:16] + dn[b, 1:17]
        cen[b] = v
        return total + v * v

    squares = lax.fori_loop(0, NB, finish_pool, jnp.zeros((16, 128), F32))
    inv = lax.rsqrt(jnp.sum(squares, axis=1, keepdims=True) / (NB * 128.0) + 1e-6)
    for c in local[2:5]:
        c.wait()

    def project(b, total):
        n = (cen[b] * inv * gain[lanes(b)].reshape(1, 128)).astype(BF16)
        normed[b] = n
        return total + dot(n, wcat[pl.ds(pl.multiple_of(b * 128, 128), 128), :], 1, 0)

    feats[fidx(me)] = lax.fori_loop(0, NB, project, jnp.zeros((16, 256), F32)).astype(BF16)

    def hop1(v):
        block = feats.at[fidx(me)]
        return remote(block, block, feat_s.at[v], feat_r.at[v], in_seq(y * 8 + lax.rem(zl + v, 4) * 2 + core))

    def hop2(v):
        block = feats.at[pl.ds(core * 16 + y * 4, 4)]
        return remote(block, block, feat_s.at[3 + v], feat_r.at[3 + v], in_seq(lax.rem(y + v, 4) * 8 + zl * 2 + core))

    def hop3(half):
        block = feats.at[pl.ds(half * 16, 16)]
        return remote(block, block, feat_s.at[0], feat_r.at[0], in_seq(partner))

    for v in (1, 2, 3):
        hop1(v).start()
    loop(EARLY, AHEAD, send_tile)
    tile_copy(15, 0, partner).start()
    tile_copy(15, 1, partner).start()
    tok_halo(0, left).start()
    tok_halo(1, right).start()

    def n_copy(g):
        return remote(normed.at[lax.rem(g, NB)], nin.at[mine], n_s.at[g], n_r.at[mine], owner(g))

    def arrived(buf, sems, k):
        remote(buf.at[k], buf.at[k], n_s.at[0], sems.at[k], owner(k)).wait_recv()

    def others(lo, hi, f):
        @pl.when(lo < hi)
        def _():
            loop(lo, jnp.clip(mine, lo, hi), f)
            loop(jnp.clip(mine + 1, lo, hi), hi, f)

    others(0, 24, lambda g: n_copy(g).start())
    for v in (1, 2, 3):
        hop1(v).wait_recv()
    for v in (1, 2, 3):
        hop2(v).start()

    for c in local[5:]:
        c.wait()

    def add_left_right(grad, f):
        accl[...] += grad * f[:, 128:][None]
        accr[...] += grad * f[:, :128][None]

    def tile(s, k, weight):
        own = jnp.concatenate(
            [pairv[:, cols(k), :].reshape(256, 128), cotv[:, cols(k), :].reshape(256, 128)], axis=1
        )
        other = jnp.concatenate([recv[s, 0].reshape(256, 128), recv[s, 1].reshape(256, 128)], axis=1)
        both = own.astype(F32) + dot(perm[...], other, 1, 0)
        here, theirs = feats[fidx(me)].astype(F32), feats[fidx(k)].astype(F32)
        outer = here[:, None, :128] * theirs[None, :, 128:] + here[:, None, 128:] * theirs[None, :, :128]
        sym = (both[:, :128] + outer.reshape(256, 128)).astype(BF16)
        cs = both[:, 128:]
        csb = cs.astype(BF16)
        pre = dot(sym, wa[...], 1, 0)
        sig = 0.5 * jnp.tanh(0.5 * pre) + 0.5
        act = pre * sig
        gpre = (dot(csb, wb[...], 1, 1) * (sig + act * (1.0 - sig))).astype(BF16)
        grad = cs + dot(gpre, wa[...], 1, 1)
        wacc[0] += dot(sym, gpre, 0, 0) * weight
        wacc[1] += dot(csb, act.astype(BF16), 0, 0) * weight
        add_left_right(grad.reshape(16, 16, 128), theirs)
        gradb = grad.astype(BF16)
        gpair[:, cols(k), :] = gradb.reshape(16, 16, 128)
        return gradb

    tile(16, me, 0.5)
    for v in (1, 2, 3):
        hop2(v).wait_recv()
    hop3(core).start()
    tile_copy(15, 0, partner).wait()
    tile_copy(15, 1, partner).wait()
    hop3(1 - core).wait_recv()
    tile(15, partner, 0.5)

    def ret_copy(s, dev):
        return remote(rbuf.at[s], gpair.at[:, cols(me), :], ret_s.at[s], ret_r.at[s], in_seq(dev))

    def owned(s):
        pl.when(s + AHEAD < 15)(lambda: send_tile(s + AHEAD))
        k = source(s)
        dev = target(s)
        tile_copy(s, 0, dev).wait_recv()
        tile_copy(s, 1, dev).wait_recv()
        gradb = tile(s, k, 1.0)
        rbuf[s] = dot(perm[...], gradb, 1, 0).astype(BF16).reshape(16, 16, 128)
        ret_copy(s, k).start()

    loop(0, 15, owned)

    for q in range(4):
        lane = slice(q * 128, q * 128 + 128)
        w3_out[q] = (wacc[0, :, lane] * scale).reshape(8, 16, 128).astype(BF16)
        w3_out[4 + q] = (wacc[1, :, lane].T * scale).reshape(8, 16, 128).astype(BF16)

    def w3_copy(g):
        return remote(w3_out.at[g - 24], w3_in.at[mine], w3_s.at[g - 24], w3_r.at[mine], owner(g))

    others(24, 32, lambda g: w3_copy(g).start())

    @pl.when(mine < 24)
    def _():
        others(0, 32, lambda k: arrived(nin, n_r, k))
        nin[mine] = normed[lax.rem(mine, NB)]

    @pl.when(mine >= 24)
    def _():
        others(0, 32, lambda k: arrived(w3_in, w3_r, k))
        w3_in[mine] = w3_out[jnp.maximum(mine - 24, 0)]
        mid[0:8] = lax.fori_loop(1, 32, lambda k, t: t + w3_in[k].astype(F32), w3_in[0].astype(F32))

    def returned(s):
        k = target(s)
        remote(rbuf.at[s], gpair.at[:, cols(k), :], ret_s.at[s], ret_r.at[s], in_seq(k)).wait_recv()
        add_left_right(gpair[:, cols(k), :].astype(F32), feats[fidx(k)].astype(F32))

    loop(0, 15, returned)
    pair_out = pltpu.make_async_copy(gpair, g_pair, loc.at[11])
    pair_out.start()

    glr_out[0] = jnp.sum(accl[...], axis=1).astype(BF16)
    glr_out[1] = jnp.sum(accr[...], axis=1).astype(BF16)

    def g_copy(g):
        return remote(glr_out.at[lax.div(g, NB)], gin.at[mine], g_s.at[g], g_r.at[mine], owner(g))

    others(0, 24, lambda g: g_copy(g).start())
    glr = jnp.concatenate([glr_out[0], glr_out[1]], axis=1)

    def grad_norm(b, carry):
        total, unused = carry
        gn = dot(glr, wcat[pl.ds(pl.multiple_of(b * 128, 128), 128), :], 1, 1)
        scaled = gn * gain[lanes(b)].reshape(1, 128)
        gpx[b, 1:17] = scaled
        mid[8, pl.ds(b, 1)] = jnp.sum(gn * cen[b] * inv, axis=0, keepdims=True) * scale
        return total + scaled * cen[b], unused

    mid[8] = jnp.zeros((16, 128), F32)
    total, _ = lax.fori_loop(0, NB, grad_norm, (jnp.zeros((16, 128), F32), 0))
    mean = jnp.sum(total, axis=1, keepdims=True) / (NB * 128.0) * inv * inv * inv

    def grad_pool(b):
        v = (gpx[b, 1:17] * inv - cen[b] * mean).astype(BF16).astype(F32)
        gpx[b, 1:17] = v
        halo_out[2, b] = v[0:1]
        halo_out[3, b] = v[15:16]

    loop(0, NB, grad_pool)
    to_left2, to_right2 = halo_pair(2)
    to_left2.start()
    to_right2.start()

    w2_out[24] = mid[8].astype(BF16)
    for g in range(25, 32):
        w2_out[g] = jnp.zeros((16, 128), BF16)
    tok_halo(0, left).wait_recv()
    tok_halo(1, right).wait_recv()

    def taps_grad(b):
        s0 = s1 = s2 = s3 = jnp.zeros((8, 128), F32)
        hi_before = tokh[1, :, lanes(b)].astype(F32)[8:16] * first
        t = tokv[0:16, lanes(b)].astype(F32)
        for p in range(16):
            here = gpx[b, p + 1 : p + 2]
            lo, hi = t[0:8], t[8:16]
            if p < 15:
                t = tokv[p * 16 + 16 : p * 16 + 32, lanes(b)].astype(F32)
                lo_after = t[0:8]
            else:
                lo_after = tokh[0, :, lanes(b)].astype(F32)[0:8] * last
            s0 = s0 + here * hi_before
            s1 = s1 + here * lo
            s2 = s2 + here * hi
            s3 = s3 + here * lo_after
            hi_before = hi
        w2_out[2 * b] = (jnp.concatenate([s0, s1], axis=0) * scale).astype(BF16)
        w2_out[2 * b + 1] = (jnp.concatenate([s2, s3], axis=0) * scale).astype(BF16)

    loop(0, NB, taps_grad)

    def w2_copy(g):
        return remote(w2_out.at[g], w2_in.at[mine], w2_s.at[g], w2_r.at[mine], owner(g))

    others(0, 32, lambda g: w2_copy(g).start())

    @pl.when(mine < 24)
    def _():
        others(0, 32, lambda k: arrived(gin, g_r, k))
        gin[mine] = glr_out[lax.div(mine, NB)]
        prod = dot(nin[...].reshape(512, 128), gin[...].reshape(512, 128), 0, 0) * scale
        mid[0:8] = prod.reshape(8, 16, 128)

    def c_copy(t, dev, slot):
        return remote(ring_out.at[t], recv_c.at[slot, 0], c_s.at[t, 0], c_r.at[slot, 0], dev)

    def c2_copy(t, dev, slot):
        return remote(ring_out.at[8], recv_c.at[slot, 1], c_s.at[t, 1], c_r.at[slot, 1], dev)

    def f_copy(slot, v, dev):
        return remote(fin.at[slot], fin.at[slot], f_s.at[v], f_r.at[slot], dev)

    def on_ring(f):
        loop(1, 8, lambda v: f(v, *ring(v)))

    ring_out[0:8] = mid[0:8].astype(BF16)
    on_ring(lambda v, t, dev: c_copy(t, dev, zz).start())
    recv_c[zz, 0] = ring_out[zz]

    others(0, 32, lambda k: arrived(w2_in, w2_r, k))
    w2_in[mine] = w2_out[mine]
    summed = lax.fori_loop(1, 32, lambda k, t: t + w2_in[k].astype(F32), w2_in[0].astype(F32))
    ring_out[8] = summed.astype(BF16)
    on_ring(lambda v, t, dev: c2_copy(t, dev, zz).start())
    recv_c[zz, 1] = ring_out[8]

    def ring_sum(k):
        return lax.fori_loop(1, 8, lambda t, a: a + recv_c[t, k].astype(F32), recv_c[0, k].astype(F32))

    on_ring(lambda v, t, dev: c_copy(t, dev, t).wait_recv())
    fin[zz] = ring_sum(0).astype(BF16)
    on_ring(lambda v, t, dev: f_copy(zz, v, dev).start())
    on_ring(lambda v, t, dev: c2_copy(t, dev, t).wait_recv())
    fin[8] = ring_sum(1).astype(BF16)
    on_ring(lambda v, t, dev: f_copy(t, v, dev).wait_recv())

    def d_copy(u, dev, g):
        return remote(fin, gat.at[g], d_s.at[u], d_r.at[u], dev)

    loop(1, 16, lambda u: d_copy(u, plane(u)[1], mine).start())
    own = pltpu.make_async_copy(fin, gat.at[mine], loc.at[13])
    own.start()

    def e_copy(u, g):
        return remote(gat.at[g], gat.at[g], e_s.at[u], e_r.at[u], in_seq(partner))

    def e_own(g):
        return remote(fin, gat.at[g], e_s.at[0], e_r.at[0], in_seq(partner))

    e_own(mine).start()
    to_left2.wait()
    to_right2.wait()

    def token_grad(b):
        k0, k1, k2, k3 = tap_parts(b)
        gpx[b, 0:1] = halo_in[3, b] * first
        gpx[b, 17:18] = halo_in[2, b] * last
        for p in range(16):
            before, here, after = gpx[b, p : p + 1], gpx[b, p + 1 : p + 2], gpx[b, p + 2 : p + 3]
            g = jnp.concatenate([here * k1 + before * k3, here * k2 + after * k0], axis=0)
            gtokv[p * 16 : p * 16 + 16, lanes(b)] = g.astype(BF16)

    loop(0, NB, token_grad)
    tok_out = pltpu.make_async_copy(gtokv, g_tokens, loc.at[12])
    tok_out.start()

    def drain_tile(s):
        dev = target(s)
        tile_copy(s, 0, dev).wait_send()
        tile_copy(s, 1, dev).wait_send()
        ret_copy(s, source(s)).wait_send()

    loop(0, 15, drain_tile)
    pair_out.wait()
    for v in (1, 2, 3):
        hop1(v).wait_send()
        hop2(v).wait_send()
    hop3(core).wait_send()
    tok_halo(0, left).wait_send()
    tok_halo(1, right).wait_send()

    def drain_features(g):
        n_copy(g).wait_send()
        g_copy(g).wait_send()

    others(0, 24, drain_features)
    others(24, 32, lambda g: w3_copy(g).wait_send())
    others(0, 32, lambda g: w2_copy(g).wait_send())
    def drain_ring(v, t, dev):
        c_copy(t, dev, zz).wait_send()
        c2_copy(t, dev, zz).wait_send()
        f_copy(zz, v, dev).wait_send()

    on_ring(drain_ring)

    def back(u):
        px, py = lax.rem(x + 4 - lax.div(u, 4), 4), lax.rem(y + 4 - lax.rem(u, 4), 4)
        return px, py

    def forward(u):
        px, py = back(u)
        g = chunk_of(px, py, core)
        d_copy(u, plane(u)[1], g).wait_recv()
        e_copy(u, g).start()

    loop(1, 16, forward)

    def finish(u):
        px, py = back(u)
        e_copy(u, chunk_of(px, py, 1 - core)).wait_recv()

    loop(0, 16, finish)

    own.wait()
    tok_out.wait()
    loop(1, 16, lambda u: d_copy(u, plane(u)[1], mine).wait_send())

    def drain_forward(u):
        px, py = back(u)
        e_copy(u, chunk_of(px, py, core)).wait_send()

    e_own(mine).wait_send()
    loop(1, 16, drain_forward)


def finish(tok_h, pair_h, gat_h, g_tokens, g_pair, g_lw, g_rw, g_taps, g_gain, g_wa, g_wb, pairv, tokv, gat, lwv, rwv, tapsv, gainv, wav, wbv, sem):
    def put(src, dst, k):
        c = pltpu.make_async_copy(src, dst, sem.at[k])
        c.start()
        return c

    weights = put(gat_h, gat, 8)
    parts = [put(pair_h.at[pl.ds(4 * q, 4)], pairv.at[pl.ds(4 * q, 4)], 9 + q) for q in range(4)]
    toks = put(tok_h, tokv, 13)
    copies = []
    for q in range(4):
        parts[q].wait()
        copies.append(put(pairv.at[pl.ds(4 * q, 4)], g_pair.at[pl.ds(4 * q, 4)], 14 + q))
    toks.wait()
    copies.append(put(tokv, g_tokens, 1))
    weights.wait()
    for b in range(NB):
        rows = slice(b * 128, b * 128 + 128)
        lwv[rows, :] = gat[b, 0:8].reshape(128, 128).astype(F32)
        rwv[rows, :] = gat[b + 12, 0:8].reshape(128, 128).astype(F32)
    copies += [put(lwv, g_lw, 2), put(rwv, g_rw, 3)]
    for q in range(4):
        lane = slice(q * 128, q * 128 + 128)
        wav[:, lane] = gat[24 + q, 0:8].reshape(128, 128).astype(F32)
        wbv[lane, :] = gat[28 + q, 0:8].reshape(128, 128).astype(F32)
    copies += [put(wav, g_wa, 4), put(wbv, g_wb, 5)]
    gains = gat[24, 8].astype(F32)
    for b in range(NB):
        rows = slice(b * 128, b * 128 + 128)
        tapsv[0:16, rows] = gat[2 * b, 8].astype(F32)
        tapsv[16:32, rows] = gat[2 * b + 1, 8].astype(F32)
        gainv[rows] = gains[b]
    copies += [put(tapsv, g_taps, 6), put(gainv, g_gain, 7)]
    for c in copies:
        c.wait()


def local(tokens, pair_in, cotangent, kernel, norm_gain, left_weight, right_weight, transition_a, transition_b):
    plen = pair_in.shape[2]
    scale = 1.0 / math.sqrt(lax.axis_size("dp") * plen * plen)
    hbm = pl.BlockSpec(memory_space=pltpu.HBM)
    dma = pltpu.SemaphoreType.DMA
    tile = (16, 16, 128)
    chunk = (9, 16, 128)
    held = pl.pallas_call(
        functools.partial(body, scale),
        out_shape=(
            jax.ShapeDtypeStruct((256, 1536), BF16),
            jax.ShapeDtypeStruct((16, 512, 128), BF16),
            jax.ShapeDtypeStruct((32,) + chunk, BF16),
        ),
        in_specs=[hbm] * 9,
        out_specs=(hbm,) * 3,
        scratch_shapes=[
            pltpu.VMEM((256, 1536), BF16),
            pltpu.VMEM((16, 512, 128), BF16),
            pltpu.VMEM((256, 1536), BF16),
            pltpu.VMEM((2, 16, 1536), BF16),
            pltpu.VMEM((16, 512, 128), BF16),
            pltpu.VMEM((16, 512, 128), BF16),
            pltpu.VMEM((17, 2) + tile, BF16),
            pltpu.VMEM((15,) + tile, BF16),
            pltpu.VMEM((32, 16, 256), BF16),
            pltpu.VMEM((256, 256), BF16),
            pltpu.VMEM((1536, 256), BF16),
            pltpu.VMEM((32, 1536), BF16),
            pltpu.VMEM((1536,), F32),
            pltpu.VMEM((128, 512), BF16),
            pltpu.VMEM((512, 128), BF16),
            pltpu.VMEM((NB, 16, 128), F32),
            pltpu.VMEM((NB, 24, 128), F32),
            pltpu.VMEM((NB, 24, 128), F32),
            pltpu.VMEM((NB, 16, 128), BF16),
            pltpu.VMEM((NB, 24, 128), F32),
            pltpu.VMEM((4, NB, 1, 128), F32),
            pltpu.VMEM((4, NB, 1, 128), F32),
            pltpu.VMEM(tile, F32),
            pltpu.VMEM(tile, F32),
            pltpu.VMEM((2, 128, 512), F32),
            pltpu.VMEM((2, 16, 128), BF16),
            pltpu.VMEM((32, 16, 128), BF16),
            pltpu.VMEM((32, 16, 128), BF16),
            pltpu.VMEM((8, 8, 16, 128), BF16),
            pltpu.VMEM((32, 8, 16, 128), BF16),
            pltpu.VMEM((32, 16, 128), BF16),
            pltpu.VMEM((32, 16, 128), BF16),
            pltpu.VMEM(chunk, F32),
            pltpu.VMEM(chunk, BF16),
            pltpu.VMEM((8, 2, 16, 128), BF16),
            pltpu.VMEM(chunk, BF16),
            dma((14,)),
            dma((16, 2)),
            dma((16, 2)),
            dma((7,)),
            dma((7,)),
            dma((15,)),
            dma((15,)),
            dma((4,)),
            dma((4,)),
            dma((2,)),
            dma((2,)),
            dma((24,)),
            dma((32,)),
            dma((24,)),
            dma((32,)),
            dma((8,)),
            dma((32,)),
            dma((32,)),
            dma((32,)),
            dma((8, 2)),
            dma((8, 2)),
            dma((8,)),
            dma((8,)),
            dma((16,)),
            dma((16,)),
            dma((16,)),
            dma((16,)),
        ],
        compiler_params=pltpu.CompilerParams(
            collective_id=0, has_side_effects=True, vmem_limit_bytes=VMEM_LIMIT
        ),
    )(
        tokens[0],
        pair_in[0],
        cotangent[0],
        kernel,
        norm_gain,
        left_weight,
        right_weight,
        transition_a,
        transition_b,
    )
    outs = pl.pallas_call(
        finish,
        out_shape=(
            jax.ShapeDtypeStruct((256, 1536), BF16),
            jax.ShapeDtypeStruct((16, 512, 128), BF16),
            jax.ShapeDtypeStruct((1536, 128), F32),
            jax.ShapeDtypeStruct((1536, 128), F32),
            jax.ShapeDtypeStruct((32, 1536), F32),
            jax.ShapeDtypeStruct((1536,), F32),
            jax.ShapeDtypeStruct((128, 512), F32),
            jax.ShapeDtypeStruct((512, 128), F32),
        ),
        in_specs=[hbm] * 3,
        out_specs=(hbm,) * 8,
        scratch_shapes=[
            pltpu.VMEM((16, 512, 128), BF16),
            pltpu.VMEM((256, 1536), BF16),
            pltpu.VMEM((32,) + chunk, BF16),
            pltpu.VMEM((1536, 128), F32),
            pltpu.VMEM((1536, 128), F32),
            pltpu.VMEM((32, 1536), F32),
            pltpu.VMEM((1536,), F32),
            pltpu.VMEM((128, 512), F32),
            pltpu.VMEM((512, 128), F32),
            dma((18,)),
        ],
        compiler_params=pltpu.CompilerParams(vmem_limit_bytes=VMEM_LIMIT),
    )(*held)
    return (outs[0][None], outs[1][None], outs[2], outs[3], outs[4], outs[5], outs[6], outs[7])


def solution(mesh):
    placed = (
        P("dp", "seq", None),
        P("dp", "seq", None, None),
        P("dp", "seq", None, None),
        P(),
        P(),
        P(),
        P(),
        P(),
        P(),
    )
    return jax.shard_map(
        local,
        mesh=mesh,
        in_specs=placed,
        out_specs=(P("dp", "seq", None), P("dp", "seq", None, None), P(), P(), P(), P(), P(), P()),
        check_vma=False,
    )
```

```python
import functools
import math

import jax
import jax.numpy as jnp
from jax import lax
from jax.experimental import pallas as pl
from jax.experimental.pallas import tpu as pltpu
from jax.sharding import PartitionSpec as P

POOL = 16
NB = 12
EARLY = 7
AHEAD = 15
VMEM_LIMIT = 58 * 1024 * 1024
F32 = jnp.float32
BF16 = jnp.bfloat16
MESH = pl.DeviceIdType.MESH


def dot(a, b, ca, cb):
    return lax.dot_general(a, b, (((ca,), (cb,)), ((), ())), preferred_element_type=F32)


def body(
    scale,
    tokens,
    pair,
    cot,
    taps_h,
    gain_h,
    lw,
    rw,
    wa_h,
    wb_h,
    g_tokens,
    g_pair,
    gat,
    gtokv,
    gpair,
    tokv,
    tokh,
    pairv,
    cotv,
    recv,
    rbuf,
    feats,
    perm,
    wcat,
    taps,
    gain,
    wa,
    wb,
    cen,
    up,
    dn,
    normed,
    gpx,
    halo_out,
    halo_in,
    accl,
    accr,
    wacc,
    glr_out,
    nin,
    gin,
    w3_out,
    w3_in,
    w2_out,
    w2_in,
    mid,
    ring_out,
    recv_c,
    fin,
    loc,
    tile_s,
    tile_r,
    feat_s,
    feat_r,
    ret_s,
    ret_r,
    halo_s,
    halo_r,
    th_s,
    th_r,
    n_s,
    n_r,
    g_s,
    g_r,
    w3_s,
    w3_r,
    w2_s,
    w2_r,
    c_s,
    c_r,
    f_s,
    f_r,
    d_s,
    d_r,
    e_s,
    e_r,
):
    dpi = lax.axis_index("dp")
    me = lax.axis_index("seq")
    x, zh = lax.div(dpi, 2), lax.rem(dpi, 2)
    chip, core = lax.div(me, 2), lax.rem(me, 2)
    y, zl = lax.div(chip, 4), lax.rem(chip, 4)
    zz = zh * 4 + zl
    partner = chip * 2 + 1 - core

    def step(s):
        return lax.div(15 - s, 4), lax.rem(15 - s, 4)

    def target(s):
        dy, dz = step(s)
        q = lax.rem(y + dy, 4) * 4 + lax.rem(zl + dz, 4)
        return q * 2 + jnp.where(q > chip, core, 1 - core)

    def source(s):
        dy, dz = step(s)
        r = lax.rem(y + 4 - dy, 4) * 4 + lax.rem(zl + 4 - dz, 4)
        return r * 2 + jnp.where(r < chip, core, 1 - core)

    def in_seq(k):
        return (dpi, k)

    def plane(u):
        px, py = lax.rem(x + lax.div(u, 4), 4), lax.rem(y + lax.rem(u, 4), 4)
        return chunk_of(px, py, core), (px * 2 + zh, py * 8 + zl * 2 + core)

    def chunk_of(px, py, pc):
        odd = lax.rem(px + py, 2)
        return jnp.where(pc == 0, px * 4 + py, 16 + (1 - odd) * 8 + px * 2 + lax.div(py, 2))

    def owner(g):
        t = lax.rem(g, 16)
        e, r = lax.div(t, 8), lax.rem(t, 8)
        rx = lax.div(r, 2)
        ry = lax.rem(r, 2) * 2 + lax.rem(1 - e + rx, 2)
        px = jnp.where(g < 16, lax.div(t, 4), rx)
        py = jnp.where(g < 16, lax.rem(t, 4), ry)
        return (px * 2 + zh, py * 8 + zl * 2 + lax.div(g, 16))

    mine = chunk_of(x, y, core)

    def ring(v):
        t = lax.rem(zz + v, 8)
        return t, (x * 2 + lax.div(t, 4), y * 8 + lax.rem(t, 4) * 2 + core)

    def remote(src, dst, ssem, rsem, dev):
        return pltpu.make_async_remote_copy(
            src_ref=src, dst_ref=dst, send_sem=ssem, recv_sem=rsem, device_id=dev, device_id_type=MESH
        )

    def cols(k):
        return pl.ds(pl.multiple_of(k * 16, 16), 16)

    def fidx(k):
        return lax.rem(k, 2) * 16 + lax.div(k, 2)

    def loop(lo, hi, f):
        def g(i, carry):
            f(i)
            return carry

        lax.fori_loop(lo, hi, g, 0)

    local = [
        pltpu.make_async_copy(tokens, tokv, loc.at[0]),
        pltpu.make_async_copy(taps_h, taps, loc.at[1]),
        pltpu.make_async_copy(gain_h, gain, loc.at[2]),
        pltpu.make_async_copy(lw, wcat.at[:, pl.ds(0, 128)], loc.at[3]),
        pltpu.make_async_copy(rw, wcat.at[:, pl.ds(128, 128)], loc.at[4]),
        pltpu.make_async_copy(wa_h, wa, loc.at[5]),
        pltpu.make_async_copy(wb_h, wb, loc.at[6]),
        pltpu.make_async_copy(pair, pairv, loc.at[7]),
        pltpu.make_async_copy(cot, cotv, loc.at[8]),
        pltpu.make_async_copy(pair.at[:, cols(me), :], recv.at[16, 0], loc.at[9]),
        pltpu.make_async_copy(cot.at[:, cols(me), :], recv.at[16, 1], loc.at[10]),
    ]
    for c in local:
        c.start()

    barrier = pltpu.get_barrier_semaphore()

    def greet(dev):
        pl.semaphore_signal(barrier, inc=1, device_id=dev, device_id_type=MESH)

    def greet_seq(s):
        greet(in_seq(target(s)))
        greet(in_seq(source(s)))

    loop(0, 15, greet_seq)
    greet(in_seq(partner))
    def greet_plane(u):
        px, py = lax.rem(x + lax.div(u, 4), 4), lax.rem(y + lax.rem(u, 4), 4)
        greet((px * 2 + zh, py * 8 + zl * 2 + core))
        greet((px * 2 + zh, py * 8 + zl * 2 + 1 - core))

    loop(4, 16, greet_plane)
    loop(0, 4, lambda v: greet((x * 2 + 1 - zh, y * 8 + v * 2 + core)))

    def tile_copy(s, k, dev):
        return remote(
            (pair, cot)[k].at[:, cols(dev), :], recv.at[s, k], tile_s.at[s, k], tile_r.at[s, k], in_seq(dev)
        )

    def send_tile(i):
        s = jnp.where((core == 1) & (i < 14), i + 1 - 2 * lax.rem(i, 2), i)
        dev = target(s)
        tile_copy(s, 0, dev).start()
        tile_copy(s, 1, dev).start()

    row = lax.broadcasted_iota(jnp.int32, (256, 256), 0)
    col = lax.broadcasted_iota(jnp.int32, (256, 256), 1)
    perm[...] = jnp.where(col == (row & 15) * 16 + (row >> 4), 1.0, 0.0).astype(BF16)
    wacc[...] = jnp.zeros_like(wacc)
    accl[...] = jnp.zeros_like(accl)
    accr[...] = jnp.zeros_like(accr)

    def lanes(b):
        return pl.ds(pl.multiple_of(b * 128, 128), 128)

    local[0].wait()
    local[1].wait()

    def tap_parts(b):
        k = taps[:, lanes(b)].astype(F32)
        return k[0:8], k[8:16], k[16:24], k[24:32]

    def pool(b):
        k0, k1, k2, k3 = tap_parts(b)
        for p in range(16):
            t = tokv[p * 16 : p * 16 + 16, lanes(b)].astype(F32)
            lo, hi = t[0:8], t[8:16]
            cen[b, p : p + 1] = jnp.sum(lo * k1 + hi * k2, axis=0, keepdims=True)
            up[b, p + 1 : p + 2] = jnp.sum(hi * k0, axis=0, keepdims=True)
            dn[b, p : p + 1] = jnp.sum(lo * k3, axis=0, keepdims=True)
        halo_out[0, b] = dn[b, 0:1]
        halo_out[1, b] = up[b, 16:17]

    loop(0, NB, pool)
    left, right = lax.rem(me + 31, 32), lax.rem(me + 1, 32)

    def halo(k, j, dev):
        return remote(halo_out.at[k], halo_in.at[k], halo_s.at[k], halo_r.at[k], in_seq(dev))

    def halo_pair(k):
        return halo(k, 0, left), halo(k + 1, 1, right)

    def tok_halo(k, dev):
        rows = pl.ds(240 * k, 16)
        return remote(tokens.at[rows, :], tokh.at[k], th_s.at[k], th_r.at[k], in_seq(dev))

    pl.semaphore_wait(barrier, 59)
    to_left, to_right = halo_pair(0)
    to_left.start()
    to_right.start()
    loop(0, EARLY, send_tile)
    to_left.wait()
    to_right.wait()
    first = jnp.where(me == 0, 0.0, 1.0)
    last = jnp.where(me == 31, 0.0, 1.0)

    def finish_pool(b, total):
        up[b, 0:1] = halo_in[1, b] * first
        dn[b, 16:17] = halo_in[0, b] * last
        v = cen[b] + up[b, 0:16] + dn[b, 1:17]
        cen[b] = v
        return total + v * v

    squares = lax.fori_loop(0, NB, finish_pool, jnp.zeros((16, 128), F32))
    inv = lax.rsqrt(jnp.sum(squares, axis=1, keepdims=True) / (NB * 128.0) + 1e-6)
    for c in local[2:5]:
        c.wait()

    def project(b, total):
        n = (cen[b] * inv * gain[lanes(b)].reshape(1, 128)).astype(BF16)
        normed[b] = n
        return total + dot(n, wcat[pl.ds(pl.multiple_of(b * 128, 128), 128), :], 1, 0)

    feats[fidx(me)] = lax.fori_loop(0, NB, project, jnp.zeros((16, 256), F32)).astype(BF16)

    def hop1(v):
        block = feats.at[fidx(me)]
        return remote(block, block, feat_s.at[v], feat_r.at[v], in_seq(y * 8 + lax.rem(zl + v, 4) * 2 + core))

    def hop2(v):
        block = feats.at[pl.ds(core * 16 + y * 4, 4)]
        return remote(block, block, feat_s.at[3 + v], feat_r.at[3 + v], in_seq(lax.rem(y + v, 4) * 8 + zl * 2 + core))

    def hop3(half):
        block = feats.at[pl.ds(half * 16, 16)]
        return remote(block, block, feat_s.at[0], feat_r.at[0], in_seq(partner))

    for v in (1, 2, 3):
        hop1(v).start()
    loop(EARLY, AHEAD, send_tile)
    tile_copy(15, 0, partner).start()
    tile_copy(15, 1, partner).start()
    tok_halo(0, left).start()
    tok_halo(1, right).start()

    def n_copy(g):
        return remote(normed.at[lax.rem(g, NB)], nin.at[mine], n_s.at[g], n_r.at[mine], owner(g))

    def arrived(buf, sems, k):
        remote(buf.at[k], buf.at[k], n_s.at[0], sems.at[k], owner(k)).wait_recv()

    def others(lo, hi, f):
        @pl.when(lo < hi)
        def _():
            loop(lo, jnp.clip(mine, lo, hi), f)
            loop(jnp.clip(mine + 1, lo, hi), hi, f)

    others(0, 24, lambda g: n_copy(g).start())
    for v in (1, 2, 3):
        hop1(v).wait_recv()
    for v in (1, 2, 3):
        hop2(v).start()

    for c in local[5:]:
        c.wait()

    def add_left_right(grad, f):
        accl[...] += grad * f[:, 128:][None]
        accr[...] += grad * f[:, :128][None]

    def tile(s, k, weight):
        own = jnp.concatenate(
            [pairv[:, cols(k), :].reshape(256, 128), cotv[:, cols(k), :].reshape(256, 128)], axis=1
        )
        other = jnp.concatenate([recv[s, 0].reshape(256, 128), recv[s, 1].reshape(256, 128)], axis=1)
        both = own.astype(F32) + dot(perm[...], other, 1, 0)
        here, theirs = feats[fidx(me)].astype(F32), feats[fidx(k)].astype(F32)
        outer = here[:, None, :128] * theirs[None, :, 128:] + here[:, None, 128:] * theirs[None, :, :128]
        sym = (both[:, :128] + outer.reshape(256, 128)).astype(BF16)
        cs = both[:, 128:]
        csb = cs.astype(BF16)
        pre = dot(sym, wa[...], 1, 0)
        sig = 0.5 * jnp.tanh(0.5 * pre) + 0.5
        act = pre * sig
        gpre = (dot(csb, wb[...], 1, 1) * (sig + act * (1.0 - sig))).astype(BF16)
        grad = cs + dot(gpre, wa[...], 1, 1)
        wacc[0] += dot(sym, gpre, 0, 0) * weight
        wacc[1] += dot(csb, act.astype(BF16), 0, 0) * weight
        add_left_right(grad.reshape(16, 16, 128), theirs)
        gradb = grad.astype(BF16)
        gpair[:, cols(k), :] = gradb.reshape(16, 16, 128)
        return gradb

    tile(16, me, 0.5)
    for v in (1, 2, 3):
        hop2(v).wait_recv()
    hop3(core).start()
    tile_copy(15, 0, partner).wait()
    tile_copy(15, 1, partner).wait()
    hop3(1 - core).wait_recv()
    tile(15, partner, 0.5)

    def ret_copy(s, dev):
        return remote(rbuf.at[s], gpair.at[:, cols(me), :], ret_s.at[s], ret_r.at[s], in_seq(dev))

    def owned(s):
        pl.when(s + AHEAD < 15)(lambda: send_tile(s + AHEAD))
        k = source(s)
        dev = target(s)
        tile_copy(s, 0, dev).wait_recv()
        tile_copy(s, 1, dev).wait_recv()
        gradb = tile(s, k, 1.0)
        rbuf[s] = dot(perm[...], gradb, 1, 0).astype(BF16).reshape(16, 16, 128)
        ret_copy(s, k).start()

    loop(0, 15, owned)

    for q in range(4):
        lane = slice(q * 128, q * 128 + 128)
        w3_out[q] = (wacc[0, :, lane] * scale).reshape(8, 16, 128).astype(BF16)
        w3_out[4 + q] = (wacc[1, :, lane].T * scale).reshape(8, 16, 128).astype(BF16)

    def w3_copy(g):
        return remote(w3_out.at[g - 24], w3_in.at[mine], w3_s.at[g - 24], w3_r.at[mine], owner(g))

    others(24, 32, lambda g: w3_copy(g).start())

    @pl.when(mine < 24)
    def _():
        others(0, 32, lambda k: arrived(nin, n_r, k))
        nin[mine] = normed[lax.rem(mine, NB)]

    def returned(s):
        k = target(s)
        remote(rbuf.at[s], gpair.at[:, cols(k), :], ret_s.at[s], ret_r.at[s], in_seq(k)).wait_recv()
        add_left_right(gpair[:, cols(k), :].astype(F32), feats[fidx(k)].astype(F32))

    loop(0, 15, returned)
    pair_out = pltpu.make_async_copy(gpair, g_pair, loc.at[11])
    pair_out.start()

    glr_out[0] = jnp.sum(accl[...], axis=1).astype(BF16)
    glr_out[1] = jnp.sum(accr[...], axis=1).astype(BF16)

    def g_copy(g):
        return remote(glr_out.at[lax.div(g, NB)], gin.at[mine], g_s.at[g], g_r.at[mine], owner(g))

    others(0, 24, lambda g: g_copy(g).start())
    glr = jnp.concatenate([glr_out[0], glr_out[1]], axis=1)

    def grad_norm(b, carry):
        total, unused = carry
        gn = dot(glr, wcat[pl.ds(pl.multiple_of(b * 128, 128), 128), :], 1, 1)
        scaled = gn * gain[lanes(b)].reshape(1, 128)
        gpx[b, 1:17] = scaled
        mid[8, pl.ds(b, 1)] = jnp.sum(gn * cen[b] * inv, axis=0, keepdims=True) * scale
        return total + scaled * cen[b], unused

    mid[8] = jnp.zeros((16, 128), F32)
    total, _ = lax.fori_loop(0, NB, grad_norm, (jnp.zeros((16, 128), F32), 0))
    mean = jnp.sum(total, axis=1, keepdims=True) / (NB * 128.0) * inv * inv * inv

    def grad_pool(b):
        v = (gpx[b, 1:17] * inv - cen[b] * mean).astype(BF16).astype(F32)
        gpx[b, 1:17] = v
        halo_out[2, b] = v[0:1]
        halo_out[3, b] = v[15:16]

    loop(0, NB, grad_pool)
    to_left2, to_right2 = halo_pair(2)
    to_left2.start()
    to_right2.start()

    w2_out[24] = mid[8].astype(BF16)
    for g in range(25, 32):
        w2_out[g] = jnp.zeros((16, 128), BF16)
    tok_halo(0, left).wait_recv()
    tok_halo(1, right).wait_recv()

    def taps_grad(b):
        s0 = s1 = s2 = s3 = jnp.zeros((8, 128), F32)
        hi_before = tokh[1, :, lanes(b)].astype(F32)[8:16] * first
        t = tokv[0:16, lanes(b)].astype(F32)
        for p in range(16):
            here = gpx[b, p + 1 : p + 2]
            lo, hi = t[0:8], t[8:16]
            if p < 15:
                t = tokv[p * 16 + 16 : p * 16 + 32, lanes(b)].astype(F32)
                lo_after = t[0:8]
            else:
                lo_after = tokh[0, :, lanes(b)].astype(F32)[0:8] * last
            s0 = s0 + here * hi_before
            s1 = s1 + here * lo
            s2 = s2 + here * hi
            s3 = s3 + here * lo_after
            hi_before = hi
        w2_out[2 * b] = (jnp.concatenate([s0, s1], axis=0) * scale).astype(BF16)
        w2_out[2 * b + 1] = (jnp.concatenate([s2, s3], axis=0) * scale).astype(BF16)

    loop(0, NB, taps_grad)

    def w2_copy(g):
        return remote(w2_out.at[g], w2_in.at[mine], w2_s.at[g], w2_r.at[mine], owner(g))

    others(0, 32, lambda g: w2_copy(g).start())

    @pl.when(mine < 24)
    def _():
        others(0, 32, lambda k: arrived(gin, g_r, k))
        gin[mine] = glr_out[lax.div(mine, NB)]
        prod = dot(nin[...].reshape(512, 128), gin[...].reshape(512, 128), 0, 0) * scale
        mid[0:8] = prod.reshape(8, 16, 128)

    @pl.when(mine >= 24)
    def _():
        others(0, 32, lambda k: arrived(w3_in, w3_r, k))
        w3_in[mine] = w3_out[jnp.maximum(mine - 24, 0)]
        mid[0:8] = lax.fori_loop(1, 32, lambda k, t: t + w3_in[k].astype(F32), w3_in[0].astype(F32))

    def c_copy(t, dev, slot):
        return remote(ring_out.at[t], recv_c.at[slot, 0], c_s.at[t, 0], c_r.at[slot, 0], dev)

    def c2_copy(t, dev, slot):
        return remote(ring_out.at[8], recv_c.at[slot, 1], c_s.at[t, 1], c_r.at[slot, 1], dev)

    def f_copy(slot, v, dev):
        return remote(fin.at[slot], fin.at[slot], f_s.at[v], f_r.at[slot], dev)

    def on_ring(f):
        loop(1, 8, lambda v: f(v, *ring(v)))

    ring_out[0:8] = mid[0:8].astype(BF16)
    on_ring(lambda v, t, dev: c_copy(t, dev, zz).start())
    recv_c[zz, 0] = ring_out[zz]

    others(0, 32, lambda k: arrived(w2_in, w2_r, k))
    w2_in[mine] = w2_out[mine]
    summed = lax.fori_loop(1, 32, lambda k, t: t + w2_in[k].astype(F32), w2_in[0].astype(F32))
    ring_out[8] = summed.astype(BF16)
    on_ring(lambda v, t, dev: c2_copy(t, dev, zz).start())
    recv_c[zz, 1] = ring_out[8]

    def ring_sum(k):
        return lax.fori_loop(1, 8, lambda t, a: a + recv_c[t, k].astype(F32), recv_c[0, k].astype(F32))

    on_ring(lambda v, t, dev: c_copy(t, dev, t).wait_recv())
    fin[zz] = ring_sum(0).astype(BF16)
    on_ring(lambda v, t, dev: f_copy(zz, v, dev).start())
    on_ring(lambda v, t, dev: c2_copy(t, dev, t).wait_recv())
    fin[8] = ring_sum(1).astype(BF16)
    on_ring(lambda v, t, dev: f_copy(t, v, dev).wait_recv())

    def d_copy(u, dev, g):
        return remote(fin, gat.at[g], d_s.at[u], d_r.at[u], dev)

    loop(1, 16, lambda u: d_copy(u, plane(u)[1], mine).start())
    own = pltpu.make_async_copy(fin, gat.at[mine], loc.at[13])
    own.start()

    def e_copy(u, g):
        return remote(gat.at[g], gat.at[g], e_s.at[u], e_r.at[u], in_seq(partner))

    def e_own(g):
        return remote(fin, gat.at[g], e_s.at[0], e_r.at[0], in_seq(partner))

    e_own(mine).start()
    to_left2.wait()
    to_right2.wait()

    def token_grad(b):
        k0, k1, k2, k3 = tap_parts(b)
        gpx[b, 0:1] = halo_in[3, b] * first
        gpx[b, 17:18] = halo_in[2, b] * last
        for p in range(16):
            before, here, after = gpx[b, p : p + 1], gpx[b, p + 1 : p + 2], gpx[b, p + 2 : p + 3]
            g = jnp.concatenate([here * k1 + before * k3, here * k2 + after * k0], axis=0)
            gtokv[p * 16 : p * 16 + 16, lanes(b)] = g.astype(BF16)

    loop(0, NB, token_grad)
    tok_out = pltpu.make_async_copy(gtokv, g_tokens, loc.at[12])
    tok_out.start()

    def drain_tile(s):
        dev = target(s)
        tile_copy(s, 0, dev).wait_send()
        tile_copy(s, 1, dev).wait_send()
        ret_copy(s, source(s)).wait_send()

    loop(0, 15, drain_tile)
    pair_out.wait()
    for v in (1, 2, 3):
        hop1(v).wait_send()
        hop2(v).wait_send()
    hop3(core).wait_send()
    tok_halo(0, left).wait_send()
    tok_halo(1, right).wait_send()

    def drain_features(g):
        n_copy(g).wait_send()
        g_copy(g).wait_send()

    others(0, 24, drain_features)
    others(24, 32, lambda g: w3_copy(g).wait_send())
    others(0, 32, lambda g: w2_copy(g).wait_send())
    def drain_ring(v, t, dev):
        c_copy(t, dev, zz).wait_send()
        c2_copy(t, dev, zz).wait_send()
        f_copy(zz, v, dev).wait_send()

    on_ring(drain_ring)

    def back(u):
        px, py = lax.rem(x + 4 - lax.div(u, 4), 4), lax.rem(y + 4 - lax.rem(u, 4), 4)
        return px, py

    def forward(u):
        px, py = back(u)
        g = chunk_of(px, py, core)
        d_copy(u, plane(u)[1], g).wait_recv()
        e_copy(u, g).start()

    loop(1, 16, forward)

    def finish(u):
        px, py = back(u)
        e_copy(u, chunk_of(px, py, 1 - core)).wait_recv()

    loop(0, 16, finish)

    own.wait()
    tok_out.wait()
    loop(1, 16, lambda u: d_copy(u, plane(u)[1], mine).wait_send())

    def drain_forward(u):
        px, py = back(u)
        e_copy(u, chunk_of(px, py, core)).wait_send()

    e_own(mine).wait_send()
    loop(1, 16, drain_forward)


def finish(tok_h, pair_h, gat_h, g_tokens, g_pair, g_lw, g_rw, g_taps, g_gain, g_wa, g_wb, pairv, tokv, gat, lwv, rwv, tapsv, gainv, wav, wbv, sem):
    def put(src, dst, k):
        c = pltpu.make_async_copy(src, dst, sem.at[k])
        c.start()
        return c

    weights = put(gat_h, gat, 8)
    parts = [put(pair_h.at[pl.ds(4 * q, 4)], pairv.at[pl.ds(4 * q, 4)], 9 + q) for q in range(4)]
    toks = put(tok_h, tokv, 13)
    copies = []
    for q in range(4):
        parts[q].wait()
        copies.append(put(pairv.at[pl.ds(4 * q, 4)], g_pair.at[pl.ds(4 * q, 4)], 14 + q))
    toks.wait()
    copies.append(put(tokv, g_tokens, 1))
    weights.wait()
    for b in range(NB):
        rows = slice(b * 128, b * 128 + 128)
        lwv[rows, :] = gat[b, 0:8].reshape(128, 128).astype(F32)
        rwv[rows, :] = gat[b + 12, 0:8].reshape(128, 128).astype(F32)
    copies += [put(lwv, g_lw, 2), put(rwv, g_rw, 3)]
    for q in range(4):
        lane = slice(q * 128, q * 128 + 128)
        wav[:, lane] = gat[24 + q, 0:8].reshape(128, 128).astype(F32)
        wbv[lane, :] = gat[28 + q, 0:8].reshape(128, 128).astype(F32)
    copies += [put(wav, g_wa, 4), put(wbv, g_wb, 5)]
    gains = gat[24, 8].astype(F32)
    for b in range(NB):
        rows = slice(b * 128, b * 128 + 128)
        tapsv[0:16, rows] = gat[2 * b, 8].astype(F32)
        tapsv[16:32, rows] = gat[2 * b + 1, 8].astype(F32)
        gainv[rows] = gains[b]
    copies += [put(tapsv, g_taps, 6), put(gainv, g_gain, 7)]
    for c in copies:
        c.wait()


def local(tokens, pair_in, cotangent, kernel, norm_gain, left_weight, right_weight, transition_a, transition_b):
    plen = pair_in.shape[2]
    scale = 1.0 / math.sqrt(lax.axis_size("dp") * plen * plen)
    hbm = pl.BlockSpec(memory_space=pltpu.HBM)
    dma = pltpu.SemaphoreType.DMA
    tile = (16, 16, 128)
    chunk = (9, 16, 128)
    held = pl.pallas_call(
        functools.partial(body, scale),
        out_shape=(
            jax.ShapeDtypeStruct((256, 1536), BF16),
            jax.ShapeDtypeStruct((16, 512, 128), BF16),
            jax.ShapeDtypeStruct((32,) + chunk, BF16),
        ),
        in_specs=[hbm] * 9,
        out_specs=(hbm,) * 3,
        scratch_shapes=[
            pltpu.VMEM((256, 1536), BF16),
            pltpu.VMEM((16, 512, 128), BF16),
            pltpu.VMEM((256, 1536), BF16),
            pltpu.VMEM((2, 16, 1536), BF16),
            pltpu.VMEM((16, 512, 128), BF16),
            pltpu.VMEM((16, 512, 128), BF16),
            pltpu.VMEM((17, 2) + tile, BF16),
            pltpu.VMEM((15,) + tile, BF16),
            pltpu.VMEM((32, 16, 256), BF16),
            pltpu.VMEM((256, 256), BF16),
            pltpu.VMEM((1536, 256), BF16),
            pltpu.VMEM((32, 1536), BF16),
            pltpu.VMEM((1536,), F32),
            pltpu.VMEM((128, 512), BF16),
            pltpu.VMEM((512, 128), BF16),
            pltpu.VMEM((NB, 16, 128), F32),
            pltpu.VMEM((NB, 24, 128), F32),
            pltpu.VMEM((NB, 24, 128), F32),
            pltpu.VMEM((NB, 16, 128), BF16),
            pltpu.VMEM((NB, 24, 128), F32),
            pltpu.VMEM((4, NB, 1, 128), F32),
            pltpu.VMEM((4, NB, 1, 128), F32),
            pltpu.VMEM(tile, F32),
            pltpu.VMEM(tile, F32),
            pltpu.VMEM((2, 128, 512), F32),
            pltpu.VMEM((2, 16, 128), BF16),
            pltpu.VMEM((32, 16, 128), BF16),
            pltpu.VMEM((32, 16, 128), BF16),
            pltpu.VMEM((8, 8, 16, 128), BF16),
            pltpu.VMEM((32, 8, 16, 128), BF16),
            pltpu.VMEM((32, 16, 128), BF16),
            pltpu.VMEM((32, 16, 128), BF16),
            pltpu.VMEM(chunk, F32),
            pltpu.VMEM(chunk, BF16),
            pltpu.VMEM((8, 2, 16, 128), BF16),
            pltpu.VMEM(chunk, BF16),
            dma((14,)),
            dma((16, 2)),
            dma((16, 2)),
            dma((7,)),
            dma((7,)),
            dma((15,)),
            dma((15,)),
            dma((4,)),
            dma((4,)),
            dma((2,)),
            dma((2,)),
            dma((24,)),
            dma((32,)),
            dma((24,)),
            dma((32,)),
            dma((8,)),
            dma((32,)),
            dma((32,)),
            dma((32,)),
            dma((8, 2)),
            dma((8, 2)),
            dma((8,)),
            dma((8,)),
            dma((16,)),
            dma((16,)),
            dma((16,)),
            dma((16,)),
        ],
        compiler_params=pltpu.CompilerParams(
            collective_id=0, has_side_effects=True, vmem_limit_bytes=VMEM_LIMIT
        ),
    )(
        tokens[0],
        pair_in[0],
        cotangent[0],
        kernel,
        norm_gain,
        left_weight,
        right_weight,
        transition_a,
        transition_b,
    )
    outs = pl.pallas_call(
        finish,
        out_shape=(
            jax.ShapeDtypeStruct((256, 1536), BF16),
            jax.ShapeDtypeStruct((16, 512, 128), BF16),
            jax.ShapeDtypeStruct((1536, 128), F32),
            jax.ShapeDtypeStruct((1536, 128), F32),
            jax.ShapeDtypeStruct((32, 1536), F32),
            jax.ShapeDtypeStruct((1536,), F32),
            jax.ShapeDtypeStruct((128, 512), F32),
            jax.ShapeDtypeStruct((512, 128), F32),
        ),
        in_specs=[hbm] * 3,
        out_specs=(hbm,) * 8,
        scratch_shapes=[
            pltpu.VMEM((16, 512, 128), BF16),
            pltpu.VMEM((256, 1536), BF16),
            pltpu.VMEM((32,) + chunk, BF16),
            pltpu.VMEM((1536, 128), F32),
            pltpu.VMEM((1536, 128), F32),
            pltpu.VMEM((32, 1536), F32),
            pltpu.VMEM((1536,), F32),
            pltpu.VMEM((128, 512), F32),
            pltpu.VMEM((512, 128), F32),
            dma((18,)),
        ],
        compiler_params=pltpu.CompilerParams(vmem_limit_bytes=VMEM_LIMIT),
    )(*held)
    return (outs[0][None], outs[1][None], outs[2], outs[3], outs[4], outs[5], outs[6], outs[7])


def solution(mesh):
    placed = (
        P("dp", "seq", None),
        P("dp", "seq", None, None),
        P("dp", "seq", None, None),
        P(),
        P(),
        P(),
        P(),
        P(),
        P(),
    )
    return jax.shard_map(
        local,
        mesh=mesh,
        in_specs=placed,
        out_specs=(P("dp", "seq", None), P("dp", "seq", None, None), P(), P(), P(), P(), P(), P()),
        check_vma=False,
    )
```
